256 devices in a mesh: gz: 8 (over x, core), gy: 32 (over y, z).
Axes of the slice: x: 4, y: 4, z: 8, core: 2. Of those that a mesh axis runs over, the one named last changes fastest.
Arguments:
- streamwise: float32 [64, 1024, 1024], P('gz', 'gy'), may hold values from -6 to 6
- spanwise: float32 [64, 1024, 1024], P('gz', 'gy'), may hold values from -6 to 6
- wall_normal: float32 [64, 1024, 1024], P('gz', 'gy'), may hold values from -6 to 6
- spacing: float32 [64], replicated, may hold values from 0.7 to 1.4
Outputs:
- pressure: float32 [64, 1024, 1024], P('gz', 'gy')
The draws below stay inside these ranges and needn't reach their ends.
All inputs are finite; a program needn't handle non-finite values.
Results may differ from the reference program's by a relative error of at most 0.0003.
Values sent between devices are 32-bit elements; how exact they have to be, the bound alone decides.
No kernel may reach another device: no remote copies, remote signals or barrier semaphores. Data moves between devices by JAX's collectives and lax.ppermute only.
A program may use at most 64 MiB of HBM per device.

```python
import math
import jax
import jax.numpy as jnp
from jax import lax

NX = 1024
NY = 1024
NZ = 64


def steps_of(key, extent, split, low, high):
    def one(position, blocks):
        draws = jax.random.uniform(jax.random.fold_in(jax.random.fold_in(key, 6), position), (blocks,), jnp.float32, low / len(split), high / len(split))
        return jnp.repeat(jnp.exp(draws), extent[position] // blocks).reshape((-1,) + (1,) * (len(extent) - position - 1))

    loudness = one(*split[0])
    for cut in split[1:]:
        loudness = loudness * one(*cut)
    return loudness


def scatter_about(rng, shape, spread, bound, pieces=(), kind=jnp.bfloat16):
    gain = steps_of(rng, shape, pieces, -0.22, 0.18) if pieces else 1.0
    values = jax.random.normal(rng, shape, jnp.float32) * spread * gain
    return jnp.minimum(jnp.maximum(values, -bound), bound).astype(kind)


def setup_inputs(seed: int = 0) -> dict:
    streams_of = jax.random.split(jax.random.key(seed), 5)
    streamwise = scatter_about(streams_of[0], (NZ, NY, NX), 1.0, 6.0, ((0, 8), (1, 32)), jnp.float32)
    spanwise = scatter_about(streams_of[1], (NZ, NY, NX), 1.0, 6.0, ((0, 8), (1, 32)), jnp.float32)
    wall_normal = scatter_about(streams_of[2], (NZ, NY, NX), 1.0, 6.0, ((0, 8), (1, 32)), jnp.float32)
    spacing = jnp.clip(jnp.exp(jax.random.uniform(streams_of[3], (NZ,), jnp.float32, math.log(0.7), math.log(1.4))), 0.7, 1.4)
    return {"streamwise": streamwise, "spanwise": spanwise, "wall_normal": wall_normal, "spacing": spacing}


screening = 0.0015

def basis(count):
    positions = jnp.arange(count, dtype=jnp.int32)[:, None]
    columns = jnp.arange(count, dtype=jnp.int32)[None, :]
    halfway = count // 2
    waves = jnp.where(columns <= halfway, columns, columns - halfway)
    phases = positions * waves % count
    angles = 2.0 * math.pi / count * phases.astype(jnp.float32)
    scaling = jnp.where((columns == 0) | (columns == halfway), 1.0, math.sqrt(2.0)) / math.sqrt(count)
    return (jnp.where(columns <= halfway, jnp.cos(angles), jnp.sin(angles)) * scaling).astype(jnp.float32)

def eigen_values(count, wave_index):
    halfway = count // 2
    waves = jnp.where(wave_index <= halfway, wave_index, wave_index - halfway)
    return 2.0 - 2.0 * jnp.cos(2.0 * math.pi / count * waves.astype(jnp.float32))

def wall_coefficients(spacing):
    gap = 0.5 * (spacing[:-1] + spacing[1:])
    nothing = jnp.zeros((1,), jnp.float32)
    lower = jnp.concatenate([nothing, 1.0 / (gap * spacing[1:])])
    upper = jnp.concatenate([1.0 / (gap * spacing[:-1]), nothing])
    return (lower, upper)

def reference(streamwise, spanwise, wall_normal, spacing):
    highest = lax.Precision.HIGHEST
    beneath = jnp.concatenate([jnp.zeros((1, NY, NX), jnp.float32), wall_normal[:-1]], axis=0)
    diverge = streamwise - jnp.roll(streamwise, 1, axis=2) + (spanwise - jnp.roll(spanwise, 1, axis=1))
    diverge = diverge + (wall_normal - beneath) / spacing[:, None, None]
    table_x = basis(NX)
    table_y = basis(NY)
    along_x = jnp.einsum('zyx,xm->zym', diverge, table_x, precision=highest)
    forcing = -jnp.einsum('zym,yk->zkm', along_x, table_y, precision=highest)
    lower, upper = wall_coefficients(spacing)
    offset = eigen_values(NY, jnp.arange(NY, dtype=jnp.int32))[:, None] + eigen_values(NX, jnp.arange(NX, dtype=jnp.int32))[None, :] + screening

    def forward(carry, inputs):
        prev_ratio, prev_value = carry
        low_coef, up_coef, rhs_row = inputs
        pivot = low_coef + up_coef + offset + low_coef * prev_ratio
        ratio = -up_coef / pivot
        value = (rhs_row + low_coef * prev_value) / pivot
        return ((ratio, value), (ratio, value))
    start = jnp.zeros((NY, NX), jnp.float32)
    final_state, (ratios, partial_values) = lax.scan(forward, (start, start), (lower, upper, forcing))

    def backward(carry, inputs):
        ratio, value = inputs
        result = value - ratio * carry
        return (result, result)
    last_state, solved = lax.scan(backward, start, (ratios, partial_values), reverse=True)
    back_y = jnp.einsum('zkm,yk->zym', solved, table_y, precision=highest)
    return jnp.einsum('zym,xm->zyx', back_y, table_x, precision=highest)
```

```python
import functools
import math

import jax
import jax.numpy as jnp
import ml_dtypes
import numpy as np
from jax import lax
from jax.experimental import pallas as pl
from jax.experimental.pallas import tpu as pltpu
from jax.sharding import PartitionSpec as P

screening = 0.0015
NX = 1024
NY = 1024
NZ = 64
GZ = 8
GY = 32
LZ = NZ // GZ
LY = NY // GY
DEV = GZ * GY
KX = NX // DEV
f32 = jnp.float32
bf16 = jnp.bfloat16


def basis(count):
    j = np.arange(count)[:, None]
    m = np.arange(count)[None, :]
    half = count // 2
    wave = np.where(m <= half, m, m - half)
    angle = 2.0 * np.pi / count * ((j * wave) % count)
    scale = np.where((m == 0) | (m == half), 1.0, math.sqrt(2.0)) / math.sqrt(count)
    return np.where(m <= half, np.cos(angle), np.sin(angle)) * scale


def eigen(count):
    m = np.arange(count)
    half = count // 2
    wave = np.where(m <= half, m, m - half)
    return 2.0 - 2.0 * np.cos(2.0 * np.pi / count * wave)


def two(x):
    hi = np.asarray(x, np.float64).astype(ml_dtypes.bfloat16)
    lo = (x - hi.astype(np.float64)).astype(ml_dtypes.bfloat16)
    return hi, lo


@functools.lru_cache(maxsize=None)
def tables():
    half = NX // 2
    tx = basis(NX)
    ex = eigen(NX)
    columns = [
        np.concatenate([np.arange(0, half + 1, 4), half + np.arange(4, half, 4)]),
        np.concatenate([np.arange(2, half, 4), half + np.arange(2, half, 4)]),
        np.arange(1, half, 2),
        half + np.arange(1, half, 2),
    ]
    parts = [tx[:256, columns[0]], tx[:256, columns[1]], tx[:512, columns[2]], tx[:512, columns[3]]]
    fx = np.concatenate(parts, axis=0)
    ix = np.concatenate([part.T for part in parts[:2]], axis=0)
    ix2 = np.concatenate([part.T for part in parts[2:]], axis=0)
    lam_x = np.stack([ex[c] for c in columns])

    sine = np.zeros((LY, LY))
    sine[0, 0] = 1.0
    m = np.arange(1, LY)
    sine[1:, 1:] = math.sqrt(2.0 / LY) * np.sin(np.pi * m[:, None] * m[None, :] / LY)
    mu = np.full((LY,), 2.0)
    mu[1:] = 2.0 - 2.0 * np.cos(np.pi * m / LY)
    kron = np.kron(np.eye(LZ), sine)
    off1 = lam_x[:, None, :] + mu[None, :, None] + screening
    q_first = sine[:, 1].copy()
    q_first[0] = 0.0
    q_last = sine[:, LY - 1].copy()
    q_last[0] = 0.0
    mask = np.ones((LY,))
    mask[0] = 0.0
    side = np.stack([np.repeat(v[:, None], 256, axis=1) for v in (q_first, q_last, mask)])

    ty = basis(NY)
    ey = eigen(NY)
    main = basis(GY)
    partner = np.zeros((GY, GY))
    for p in range(1, GY // 2):
        partner[:, p] = main[:, GY // 2 + p]
        partner[:, GY // 2 + p] = main[:, p]
    wave = np.where(np.arange(NY) <= NY // 2, np.arange(NY), np.arange(NY) - NY // 2)
    is_cos = np.arange(NY) <= NY // 2
    fold = wave % GY
    fold = np.minimum(fold, GY - fold)
    order = np.zeros((GY, GY), np.int64)
    for p in range(GY):
        if p in (0, GY // 2):
            order[:, p] = np.nonzero(fold == p)[0]
        elif p < GY // 2:
            order[:, p] = np.nonzero((fold == p) & is_cos)[0]
        else:
            order[:, p] = np.nonzero((fold == p - GY // 2) & ~is_cos)[0]
    shaped = ty.reshape(GY, LY, NY)[:, :, order]
    a_y = np.einsum("bvjp,bp->vjp", shaped, main)
    b_y = np.einsum("bvjp,bp->vjp", shaped, partner)
    a_m = np.einsum("mv,vjp->mjp", sine, a_y)
    b_m = np.einsum("mv,vjp->mjp", sine, b_y)
    a_m = np.tile(a_m, (1, 1, KX))
    b_m = np.tile(b_m, (1, 1, KX))
    lam_y = np.tile(ey[order], (1, KX)) + screening
    lam_d = np.repeat(lam_x.T, GY, axis=1)
    spread = np.eye(KX)
    dft = np.concatenate([np.kron(spread, main), np.kron(spread, partner)], axis=1)
    as32 = lambda x: np.ascontiguousarray(x, np.float32)
    return dict(
        fx=two(fx),
        ix=two(ix),
        ix2=two(ix2),
        kron=two(kron),
        sine=two(sine),
        off1=as32(off1),
        side=as32(side),
        dft=two(dft),
        idft=two(dft.T),
        fwd=as32(np.stack([a_m, b_m])),
        inv=as32(np.stack([a_m, b_m]).transpose(0, 2, 1, 3)),
        lam_y=as32(lam_y),
        lam_d=as32(lam_d),
    )


def split(x):
    hi = x.astype(bf16)
    return hi, (x - hi.astype(f32)).astype(bf16)


def dot(a, b):
    return lax.dot_general(a, b, (((1,), (0,)), ((), ())), preferred_element_type=f32)


def dot3(a, b):
    return dot(a[0], b[0]) + (dot(a[0], b[1]) + dot(a[1], b[0]))


def wall_rows(spacing, width):
    first = lax.axis_index("gz") * LZ
    inside = first + LZ < NZ
    heights = [jnp.full((1, width), spacing[first + t], f32) for t in range(LZ)]
    above = jnp.full((1, width), spacing[jnp.minimum(first + LZ, NZ - 1)], f32)
    heights.append(above)
    gaps = [0.5 * (heights[t] + heights[t + 1]) for t in range(LZ)]
    keep = jnp.where(inside, 1.0, 0.0).astype(f32)
    lower = [None] + [1.0 / (gaps[t - 1] * heights[t]) for t in range(1, LZ + 1)]
    upper = [1.0 / (gaps[t] * heights[t]) for t in range(LZ)]
    inverse = [1.0 / heights[t] for t in range(LZ + 1)]
    lower[LZ] = lower[LZ] * keep
    upper[LZ - 1] = upper[LZ - 1] * keep
    inverse[LZ] = inverse[LZ] * keep
    return lower, upper, inverse


def block_pivots(off, mask, lower, upper):
    pivots = [None] * LZ
    for t in range(1, LZ):
        diagonal = off + (lower[t] + upper[t])
        if t > 1:
            diagonal = diagonal - (lower[t] * upper[t - 1]) * pivots[t - 1]
        pivots[t] = mask / diagonal
    return pivots


def block_solve(right, pivots, lower, upper):
    value = [None] * LZ
    for t in range(1, LZ):
        term = right[t] if t == 1 else right[t] + lower[t] * value[t - 1]
        value[t] = term * pivots[t]
    for t in range(LZ - 2, 0, -1):
        value[t] = value[t] + upper[t] * pivots[t] * value[t + 1]
    return value


def eliminate(
    spacing, stream, span, wall, fx_hi, fx_lo, kron_hi, kron_lo, sine_hi, sine_lo, off1, side,
    message, kept, part_hi, part_lo, ends,
):
    lower, upper, inverse = wall_rows(spacing, NX)
    rows = lax.broadcasted_iota(jnp.int32, (LY, NX), 0)
    for t in range(LZ + 2):
        if t < LZ:
            u = stream[t]
            v = span[t]
            w = wall[t]
            shifted = jnp.where(rows == 0, 0.0, pltpu.roll(v, 1, axis=0))
            d = (pltpu.roll(u, 1, axis=1) - u) + (shifted - v)
            d = d - w * inverse[t] if t == 0 else d + (wall[t - 1] - w) * inverse[t]
        elif t == LZ:
            d = wall[LZ - 1] * inverse[LZ]
        else:
            d = jnp.concatenate([span[z, LY - 1 :, :] for z in range(LZ)] + [jnp.zeros((8, NX), f32)], axis=0)
        even = d[:, :512] + d[:, 512:]
        odd = d[:, :512] - d[:, 512:]
        here = pl.ds(t * LY, d.shape[0])
        for first, piece in ((0, even[:, :256] + even[:, 256:]), (256, even[:, :256] - even[:, 256:]), (512, odd)):
            hi, lo = split(piece)
            part_hi[here, first : first + piece.shape[1]] = hi
            part_lo[here, first : first + piece.shape[1]] = lo
    lower, upper, inverse = wall_rows(spacing, 256)
    q_first, q_last, mask = side[0], side[1], side[2]
    for i in range(KX):
        cols = ((0, 256), (256, 512), (512, 1024), (512, 1024))[i]
        deep = ((0, 256), (256, 512), (512, 1024), (1024, 1536))[i]
        a = (part_hi[:, cols[0] : cols[1]], part_lo[:, cols[0] : cols[1]])
        b = (fx_hi[deep[0] : deep[1], :], fx_lo[deep[0] : deep[1], :])
        lines = dot3(a, b)
        cells = dot3((kron_hi[...], kron_lo[...]), split(lines[: LZ * LY]))
        crown = dot3((sine_hi[...], sine_lo[...]), split(lines[LZ * LY : (LZ + 1) * LY]))
        edge = lines[(LZ + 1) * LY : (LZ + 1) * LY + LZ]
        kept[i] = cells
        layers = [cells[t * LY : (t + 1) * LY] for t in range(LZ)]
        pivots = block_pivots(off1[i], mask, lower, upper)
        inner = block_solve(layers, pivots, lower, upper)
        ends[i * LY : (i + 1) * LY, :] = layers[0] + upper[0] * inner[1]
        ends[128 + i * LY : 128 + (i + 1) * LY, :] = crown + lower[LZ] * inner[LZ - 1]
        own = [jnp.zeros((1, 256), f32)]
        following = [jnp.zeros((1, 256), f32)]
        for t in range(1, LZ):
            own.append(layers[t][:1] + jnp.sum(inner[t] * q_first, axis=0, keepdims=True))
            following.append(jnp.sum(inner[t] * q_last, axis=0, keepdims=True))
        ends[256 + i * LZ : 256 + (i + 1) * LZ, :] = jnp.concatenate(own, axis=0)
        ends[320 + i * LZ : 320 + (i + 1) * LZ, :] = edge + jnp.concatenate(following, axis=0)
    ends[256 + KX * LZ : 320, :] = jnp.zeros((64 - KX * LZ, 256), f32)
    ends[320 + KX * LZ : 384, :] = jnp.zeros((64 - KX * LZ, 256), f32)
    for r in range(3):
        message[pl.ds(r, DEV, stride=3), :] = ends[128 * r : 128 * (r + 1), :].T


def interface(
    spacing, arrived, dft_hi, dft_lo, idft_hi, idft_lo, fwd, inv, lam_y, lam_d,
    reply, pivot, value, low, up, spec, lines, top, back,
):
    me = lax.axis_index("gz") * GY + lax.axis_index("gy")
    for z in range(NZ):
        low[z : z + 1, :] = jnp.full((1, 128), spacing[z], f32)
    heights = low[...]
    layer = lax.broadcasted_iota(jnp.int32, (NZ, 128), 0)
    gap = 0.5 * (heights + pltpu.roll(heights, NZ - 1, axis=0))
    upper_all = jnp.where(layer == NZ - 1, 0.0, 1.0 / (gap * heights))
    lower_all = jnp.where(layer == 0, 0.0, 1.0 / (pltpu.roll(gap, 1, axis=0) * heights))
    low[...] = lower_all
    up[...] = upper_all
    off = lam_y[...] + lam_d[pl.ds(me, 1), :]
    half = NZ // 2
    for s in range(half):
        for z in (s, NZ - 1 - s):
            diagonal = off + (low[z : z + 1, :] + up[z : z + 1, :])
            if s > 0:
                if z < half:
                    cross = low[z : z + 1, :] * up[z - 1 : z, :]
                    diagonal = diagonal - cross * pivot[z - 1]
                else:
                    cross = up[z : z + 1, :] * low[z + 1 : z + 2, :]
                    diagonal = diagonal - cross * pivot[z + 1]
            pivot[z] = 1.0 / diagonal
    lane = lax.broadcasted_iota(jnp.int32, (GY, 128), 1)
    field = [arrived[pl.ds(96 * a, GY, stride=3), :] for a in range(GZ)]
    for a in range(1, GZ):
        field[a] = field[a] + arrived[pl.ds(96 * (a - 1) + 1, GY, stride=3), :]
    for g in range(2):
        blocks = []
        for i in range(KX):
            block = None
            for k in range(4):
                moved = pltpu.roll(field[4 * g + k], (32 * (k - i)) % 128, axis=1)
                block = moved if block is None else jnp.where(lane // 32 == k, moved, block)
            blocks.append(block)
        stacked = jnp.concatenate(blocks, axis=0).T
        spec[128 * g : 128 * (g + 1), :] = dot3(split(stacked), (dft_hi[...], dft_lo[...]))
    sides = []
    for a in range(GZ):
        rest = arrived[pl.ds(96 * a + 2, GY, stride=3), :]
        sides.append(rest + pltpu.roll(pltpu.roll(rest, 64, axis=1), 1, axis=0))
    blocks = []
    for i in range(KX):
        block = jnp.zeros((GY, 128), f32)
        for a in range(GZ):
            moved = pltpu.roll(sides[a], (8 * (a - i)) % 128, axis=1)
            block = jnp.where(lane // 8 == a, moved, block)
        blocks.append(block)
    stacked = jnp.concatenate(blocks, axis=0).T[:NZ]
    lines[...] = dot3(split(stacked), (dft_hi[:, :128], dft_lo[:, :128]))
    for g in range(2):
        total = [jnp.zeros((GY, 128), f32)] * 4
        for m in range(LY):
            c_main = fwd[0, m]
            c_partner = fwd[1, m]
            for k in range(4):
                row = 128 * g + 32 * k + m
                total[k] = total[k] + c_main * spec[row : row + 1, :128] + c_partner * spec[row : row + 1, 128:]
        for k in range(4):
            top[4 * g + k] = total[k]
    weight = fwd[0, 0]
    for s in range(half):
        for z in (s, NZ - 1 - s):
            right = weight * lines[z : z + 1, :]
            if z % LZ == 0:
                right = right + top[z // LZ]
            if s > 0:
                if z < half:
                    right = right + low[z : z + 1, :] * value[z - 1]
                else:
                    right = right + up[z : z + 1, :] * value[z + 1]
            value[z] = right * pivot[z]
    alpha = up[half - 1 : half, :] * pivot[half - 1]
    beta = low[half : half + 1, :] * pivot[half]
    below = (value[half - 1] + alpha * value[half]) / (1.0 - alpha * beta)
    above = value[half] + beta * below
    for s in range(half):
        for z in (half - 1 - s, half + s):
            if z < half:
                if s > 0:
                    below = value[z] + up[z : z + 1, :] * pivot[z] * below
                now = below
            else:
                if s > 0:
                    above = value[z] + low[z : z + 1, :] * pivot[z] * above
                now = above
            lines[z : z + 1, :] = jnp.sum(now * weight, axis=0, keepdims=True)
            if z % LZ == 0:
                top[z // LZ] = now
    for g in range(2):
        total = [jnp.zeros((LY, 128), f32)] * 4
        other = [jnp.zeros((LY, 128), f32)] * 4
        for j in range(GY):
            c_main = inv[0, j]
            c_partner = inv[1, j]
            for k in range(4):
                row = top[4 * g + k, j : j + 1, :]
                total[k] = total[k] + c_main * row
                other[k] = other[k] + c_partner * row
        for k in range(4):
            spec[128 * g + 32 * k : 128 * g + 32 * (k + 1), :128] = total[k]
            spec[128 * g + 32 * k : 128 * g + 32 * (k + 1), 128:] = other[k]
    for g in range(2):
        back[...] = dot3(split(spec[128 * g : 128 * (g + 1), :]), (idft_hi[...], idft_lo[...])).T
        for k in range(4):
            block = None
            for i in range(KX):
                moved = pltpu.roll(back[32 * i : 32 * (i + 1), :], (32 * (i - k)) % 128, axis=1)
                block = moved if block is None else jnp.where(lane // 32 == i, moved, block)
            a = 4 * g + k
            reply[pl.ds(96 * a, GY, stride=3), :] = block
            if a > 0:
                reply[pl.ds(96 * (a - 1) + 1, GY, stride=3), :] = block
    reply[pl.ds(96 * (GZ - 1) + 1, GY, stride=3), :] = jnp.zeros((GY, 128), f32)
    rest = dot3(split(lines[...]), (idft_hi[:128, :], idft_lo[:128, :]))
    back[...] = jnp.concatenate([rest, rest], axis=0).T
    pieces = []
    for i in range(KX):
        piece = back[32 * i : 32 * (i + 1), :]
        pieces.append(jnp.where(lane < 64, piece, pltpu.roll(piece, GY - 1, axis=0)))
    for a in range(GZ):
        block = jnp.zeros((GY, 128), f32)
        for i in range(KX):
            moved = pltpu.roll(pieces[i], (8 * (i - a)) % 128, axis=1)
            block = jnp.where((lane % 64) // 8 == i, moved, block)
        reply[pl.ds(96 * a + 2, GY, stride=3), :] = block


def restore(
    spacing, arrived, kept, ix_hi, ix_lo, ix2_hi, ix2_lo, kron_hi, kron_lo, off1, side, pressure, ends,
):
    lower, upper, _ = wall_rows(spacing, 256)
    q_first, q_last, mask = side[0], side[1], side[2]
    for r in range(3):
        ends[128 * r : 128 * (r + 1), :] = arrived[pl.ds(r, DEV, stride=3), :].T
    halves = []
    odd = None
    for i in range(KX):
        floor = ends[i * LY : (i + 1) * LY, :]
        ceiling = ends[128 + i * LY : 128 + (i + 1) * LY, :]
        pivots = block_pivots(off1[i], mask, lower, upper)
        right = [None] * LZ
        near = [None] * LZ
        for t in range(1, LZ):
            near[t] = ends[256 + i * LZ + t : 256 + i * LZ + t + 1, :]
            far = ends[320 + i * LZ + t : 320 + i * LZ + t + 1, :]
            right[t] = kept[i, t * LY : (t + 1) * LY, :] + (q_first * near[t] + q_last * far)
        right[1] = right[1] + lower[1] * floor
        right[LZ - 1] = right[LZ - 1] + upper[LZ - 1] * ceiling
        inner = block_solve(right, pivots, lower, upper)
        layers = [floor] + [inner[t] + (1.0 - mask) * near[t] for t in range(1, LZ)]
        modes = jnp.concatenate(layers, axis=0)
        lines = split(dot3((kron_hi[...], kron_lo[...]), split(modes)))
        if i < 2:
            halves.append(dot3(lines, (ix_hi[256 * i : 256 * (i + 1), :], ix_lo[256 * i : 256 * (i + 1), :])))
        else:
            k = i - 2
            term = dot3(lines, (ix2_hi[256 * k : 256 * (k + 1), :], ix2_lo[256 * k : 256 * (k + 1), :]))
            odd = term if odd is None else odd + term
    first = halves[0] + halves[1]
    second = halves[0] - halves[1]
    for q, piece in ((0, first + odd[:, :256]), (1, second + odd[:, 256:]), (2, first - odd[:, :256]), (3, second - odd[:, 256:])):
        for t in range(LZ):
            pressure[t, :, 256 * q : 256 * (q + 1)] = piece[t * LY : (t + 1) * LY, :]


def on_device(streamwise, spanwise, wall_normal, spacing):
    table = tables()
    as_array = lambda name: [jnp.asarray(part) for part in table[name]]
    smem = pl.BlockSpec(memory_space=pltpu.SMEM)
    vmem = pl.BlockSpec(memory_space=pltpu.VMEM)
    params = pltpu.CompilerParams(vmem_limit_bytes=50 * 2**20)
    shape = jax.ShapeDtypeStruct
    fx, ix, ix2, kron, sine = (as_array(name) for name in ("fx", "ix", "ix2", "kron", "sine"))
    dft, idft = as_array("dft"), as_array("idft")
    off1, side, fwd, inv, lam_y, lam_d = (
        jnp.asarray(table[name]) for name in ("off1", "side", "fwd", "inv", "lam_y", "lam_d")
    )
    message, kept = pl.pallas_call(
        eliminate,
        out_shape=(shape((3 * DEV, 128), f32), shape((KX, LZ * LY, 256), f32)),
        in_specs=[smem] + [vmem] * 11,
        out_specs=(vmem, vmem),
        scratch_shapes=[
            pltpu.VMEM(((LZ + 1) * LY + 16, NX), bf16),
            pltpu.VMEM(((LZ + 1) * LY + 16, NX), bf16),
            pltpu.VMEM((384, 256), f32),
        ],
        compiler_params=params,
        name="eliminate",
    )(spacing, streamwise, spanwise, wall_normal, *fx, *kron, *sine, off1, side)
    axes = ("gz", "gy")
    trade = lambda x: lax.all_to_all(
        x.reshape(DEV, 1, 384), axes, split_axis=0, concat_axis=0, tiled=True
    ).reshape(3 * DEV, 128)
    arrived = trade(message)
    reply = pl.pallas_call(
        interface,
        out_shape=shape((3 * DEV, 128), f32),
        in_specs=[smem] + [vmem] * 9,
        out_specs=vmem,
        scratch_shapes=[
            pltpu.VMEM((NZ, GY, 128), f32),
            pltpu.VMEM((NZ, GY, 128), f32),
            pltpu.VMEM((NZ, 128), f32),
            pltpu.VMEM((NZ, 128), f32),
            pltpu.VMEM((256, 256), f32),
            pltpu.VMEM((NZ, 128), f32),
            pltpu.VMEM((GZ, GY, 128), f32),
            pltpu.VMEM((128, 128), f32),
        ],
        compiler_params=params,
        name="interface",
    )(spacing, arrived, *dft, *idft, fwd, inv, lam_y, lam_d)
    answered = trade(reply)
    return pl.pallas_call(
        restore,
        out_shape=shape((LZ, LY, NX), f32),
        in_specs=[smem] + [vmem] * 10,
        out_specs=vmem,
        scratch_shapes=[pltpu.VMEM((384, 256), f32)],
        compiler_params=params,
        name="restore",
    )(spacing, answered, kept, *ix, *ix2, *kron, off1, side)


def solution(mesh):
    placed = (P("gz", "gy", None), P("gz", "gy", None), P("gz", "gy", None), P())
    return jax.shard_map(
        on_device, mesh=mesh, in_specs=placed, out_specs=P("gz", "gy", None), check_vma=False
    )
```

```python
import functools
import math

import jax
import jax.numpy as jnp
import ml_dtypes
import numpy as np
from jax import lax
from jax.experimental import pallas as pl
from jax.experimental.pallas import tpu as pltpu
from jax.sharding import PartitionSpec as P

screening = 0.0015
NX = 1024
NY = 1024
NZ = 64
GZ = 8
GY = 32
LZ = NZ // GZ
LY = NY // GY
DEV = GZ * GY
KX = NX // DEV
SMALL = 144
SHARED = 512 + 3 * SMALL
FORWARD = SHARED + 8 * 256
BACKWARD = FORWARD + 8 * 256
SLABS = BACKWARD + 512
LEAF = GY + DEV
BOOK = LEAF + 4 * GY * LY
f32 = jnp.float32
bf16 = jnp.bfloat16


def basis(count):
    j = np.arange(count)[:, None]
    m = np.arange(count)[None, :]
    half = count // 2
    wave = np.where(m <= half, m, m - half)
    angle = 2.0 * np.pi / count * ((j * wave) % count)
    scale = np.where((m == 0) | (m == half), 1.0, math.sqrt(2.0)) / math.sqrt(count)
    return np.where(m <= half, np.cos(angle), np.sin(angle)) * scale


def eigen(count):
    m = np.arange(count)
    half = count // 2
    wave = np.where(m <= half, m, m - half)
    return 2.0 - 2.0 * np.cos(2.0 * np.pi / count * wave)


def two(x):
    hi = np.asarray(x, np.float64).astype(ml_dtypes.bfloat16)
    lo = (x - hi.astype(np.float64)).astype(ml_dtypes.bfloat16)
    return hi, lo


@functools.lru_cache(maxsize=None)
def tables():
    half = NX // 2
    tx = basis(NX)
    ex = eigen(NX)
    columns = [
        np.concatenate([np.arange(0, half + 1, 4), half + np.arange(4, half, 4)]),
        np.concatenate([np.arange(2, half, 4), half + np.arange(2, half, 4)]),
    ]
    quarter = np.arange(256)
    turn = 2.0 * np.pi / NX * (quarter[:, None] * (4 * quarter[None, :] + 1) % NX)
    waves = math.sqrt(2.0 / NX) * np.cos(turn), math.sqrt(2.0 / NX) * np.sin(turn)
    parts = [tx[:256, columns[0]], tx[:256, columns[1]], *waves]
    lam_odd = 2.0 - 2.0 * np.cos(2.0 * np.pi / NX * (4 * quarter + 1))
    lam_x = np.stack([ex[columns[0]], ex[columns[1]], lam_odd, lam_odd])

    sine = np.zeros((LY, LY))
    sine[0, 0] = 1.0
    m = np.arange(1, LY)
    sine[1:, 1:] = math.sqrt(2.0 / LY) * np.sin(np.pi * m[:, None] * m[None, :] / LY)
    mu = np.full((LY,), 2.0)
    mu[1:] = 2.0 - 2.0 * np.cos(np.pi * m / LY)
    kron = np.kron(np.eye(LZ), sine)
    q_first = sine[:, 1].copy()
    q_first[0] = 0.0
    q_last = sine[:, LY - 1].copy()
    q_last[0] = 0.0
    mask = np.ones((LY,))
    mask[0] = 0.0
    side = np.stack([np.repeat(v[:, None], 256, axis=1) for v in (q_first, q_last, mask)])
    small = np.zeros((SMALL, 256))
    small[:KX] = lam_x
    small[16 : 16 + 3 * LY] = side.reshape(3 * LY, 256)
    small[16 + 3 * LY :] = mu[:, None] + screening
    rest, thirds = small.astype(np.float32).astype(np.float64), []
    for _ in range(3):
        thirds.append(rest.astype(ml_dtypes.bfloat16))
        rest = rest - thirds[-1].astype(np.float64)
    pack = [*two(kron), *thirds]
    for part in parts:
        pack += two(part)
    for part in parts:
        pack += two(part.T)

    ty = basis(NY)
    ey = eigen(NY)
    main = basis(GY)
    partner = np.zeros((GY, GY))
    for p in range(1, GY // 2):
        partner[:, p] = main[:, GY // 2 + p]
        partner[:, GY // 2 + p] = main[:, p]
    wave = np.where(np.arange(NY) <= NY // 2, np.arange(NY), np.arange(NY) - NY // 2)
    is_cos = np.arange(NY) <= NY // 2
    fold = wave % GY
    fold = np.minimum(fold, GY - fold)
    order = np.zeros((GY, GY), np.int64)
    for p in range(GY):
        if p in (0, GY // 2):
            order[:, p] = np.nonzero(fold == p)[0]
        elif p < GY // 2:
            order[:, p] = np.nonzero((fold == p) & is_cos)[0]
        else:
            order[:, p] = np.nonzero((fold == p - GY // 2) & ~is_cos)[0]
    shaped = ty.reshape(GY, LY, NY)[:, :, order]
    a_y = np.einsum("bvjp,bp->vjp", shaped, main)
    b_y = np.einsum("bvjp,bp->vjp", shaped, partner)
    a_m = np.einsum("mv,vjp->mjp", sine, a_y)
    b_m = np.einsum("mv,vjp->mjp", sine, b_y)
    a_m = np.tile(a_m, (1, 1, KX))
    b_m = np.tile(b_m, (1, 1, KX))
    lam_y = np.tile(ey[order], (1, KX)) + screening
    lam_d = np.repeat(lam_x.T, GY, axis=1)
    spread = np.eye(KX)
    dft = np.concatenate([np.kron(spread, main), np.kron(spread, partner)], axis=1)
    pack += two(dft)
    pack.append(np.concatenate(two(dft.T), axis=1))
    pack = np.concatenate(pack, axis=0)
    assert pack.shape == (SLABS, 256)
    later = pack[FORWARD:BACKWARD]
    both = np.stack([a_m, b_m])
    book = [lam_y, lam_d, both, both.transpose(0, 2, 1, 3)]
    book = np.concatenate([part.reshape(-1, 128) for part in book], axis=0).astype(np.float32)
    assert book.shape == (BOOK, 128)
    return pack, book, later


def split(x):
    hi = x.astype(bf16)
    return hi, (x - hi.astype(f32)).astype(bf16)


def dot(a, b):
    return lax.dot_general(a, b, (((1,), (0,)), ((), ())), preferred_element_type=f32)


def dot3(a, b):
    return dot(a[0], b[0]) + (dot(a[0], b[1]) + dot(a[1], b[0]))


def wall_rows(rows, width):
    first = lax.axis_index("gz") * LZ
    inside = first + LZ < NZ
    places = [first + t for t in range(LZ)] + [jnp.minimum(first + LZ, NZ - 1)]
    heights = [jnp.concatenate([rows[pl.ds(place, 1), :]] * (width // 128), axis=1) for place in places]
    gaps = [0.5 * (heights[t] + heights[t + 1]) for t in range(LZ)]
    keep = jnp.where(inside, 1.0, 0.0).astype(f32)
    lower = [None] + [1.0 / (gaps[t - 1] * heights[t]) for t in range(1, LZ + 1)]
    upper = [1.0 / (gaps[t] * heights[t]) for t in range(LZ)]
    inverse = [1.0 / heights[t] for t in range(LZ + 1)]
    lower[LZ] = lower[LZ] * keep
    upper[LZ - 1] = upper[LZ - 1] * keep
    inverse[LZ] = inverse[LZ] * keep
    return lower, upper, inverse


def block_pivots(off, mask, lower, upper):
    pivots = [None] * LZ
    for t in range(1, LZ):
        diagonal = off + (lower[t] + upper[t])
        if t > 1:
            diagonal = diagonal - (lower[t] * upper[t - 1]) * pivots[t - 1]
        pivots[t] = mask / diagonal
    return pivots


def block_solve(right, pivots, lower, upper):
    value = [None] * LZ
    for t in range(1, LZ):
        term = right[t] if t == 1 else right[t] + lower[t] * value[t - 1]
        value[t] = term * pivots[t]
    for t in range(LZ - 2, 0, -1):
        value[t] = value[t] + upper[t] * pivots[t] * value[t + 1]
    return value


def eliminate(
    spacing_in, stream_in, span_in, wall_in, pack_in, book_in,
    message, kept, heights, book, slabs, low, up, pivot, block, shared,
    spacing, stream, span, wall, pack, part_hi, part_lo, ends, cell_sem, table_sem,
):
    first_copy = pltpu.make_async_copy(spacing_in, spacing, table_sem.at[0])
    first_copy.start()
    leaf = pltpu.make_async_copy(book_in.at[pl.ds(0, LEAF)], book.at[pl.ds(0, LEAF)], table_sem.at[4])
    leaf.start()
    copies = []
    for t in range(0, LZ, 2):
        here = pl.ds(t, 2)
        trio = [
            pltpu.make_async_copy(source.at[here], target.at[here], cell_sem.at[t // 2, k])
            for k, (source, target) in enumerate(((stream_in, stream), (span_in, span), (wall_in, wall)))
        ]
        for copy in trio:
            copy.start()
        copies.append(trio)
    table_copies = []
    moves = (
        (pack_in.at[pl.ds(0, SHARED)], shared),
        (pack_in.at[pl.ds(SHARED, 1024)], pack.at[pl.ds(0, 1024)]),
        (pack_in.at[pl.ds(SHARED + 1024, 1024)], pack.at[pl.ds(1024, 1024)]),
    )
    for k, (source, target) in enumerate(moves):
        table_copies.append(pltpu.make_async_copy(source, target, table_sem.at[k + 1]))
        table_copies[-1].start()
    ahead = [
        pltpu.make_async_copy(pack_in.at[pl.ds(BACKWARD, 512)], slabs, table_sem.at[5]),
        pltpu.make_async_copy(
            book_in.at[pl.ds(LEAF, BOOK - LEAF)], book.at[pl.ds(LEAF, BOOK - LEAF)], table_sem.at[6]
        ),
    ]
    for copy in ahead:
        copy.start()
    first_copy.wait()
    for z in range(NZ):
        heights[z : z + 1, :] = jnp.full((1, 128), spacing[z], f32)
    tall = heights[...]
    layer = lax.broadcasted_iota(jnp.int32, (NZ, 128), 0)
    gap = 0.5 * (tall + pltpu.roll(tall, NZ - 1, axis=0))
    low[...] = jnp.where(layer == 0, 0.0, 1.0 / (pltpu.roll(gap, 1, axis=0) * tall))
    up[...] = jnp.where(layer == NZ - 1, 0.0, 1.0 / (gap * tall))
    leaf.wait()
    me = lax.axis_index("gy") * GZ + lax.axis_index("gz")
    off = book[pl.ds(0, GY), :] + book[pl.ds(GY + me, 1), :]
    half = NZ // 2
    last = [None, None]

    def wall_step(s):
        for side, z in enumerate((s, NZ - 1 - s)):
            diagonal = off + (low[z : z + 1, :] + up[z : z + 1, :])
            if s > 0 and side == 0:
                diagonal = diagonal - (low[z : z + 1, :] * up[z - 1 : z, :]) * last[0]
            if s > 0 and side == 1:
                diagonal = diagonal - (up[z : z + 1, :] * low[z + 1 : z + 2, :]) * last[1]
            last[side] = 1.0 / diagonal
            pivot[z] = last[side]

    lower, upper, inverse = wall_rows(heights, NX)
    rows = lax.broadcasted_iota(jnp.int32, (LY, NX), 0)
    for t in range(LZ + 2):
        if t < LZ:
            if t % 2 == 0:
                for copy in copies[t // 2]:
                    copy.wait()
            u = stream[t]
            v = span[t]
            w = wall[t]
            shifted = jnp.where(rows == 0, 0.0, pltpu.roll(v, 1, axis=0))
            d = (pltpu.roll(u, 1, axis=1) - u) + (shifted - v)
            d = d - w * inverse[t] if t == 0 else d + (wall[t - 1] - w) * inverse[t]
        elif t == LZ:
            d = wall[LZ - 1] * inverse[LZ]
        else:
            d = jnp.concatenate([span[z, LY - 1 :, :] for z in range(LZ)] + [jnp.zeros((8, NX), f32)], axis=0)
        even = d[:, :512] + d[:, 512:]
        odd = d[:, :512] - d[:, 512:]
        here = pl.ds(t * LY, d.shape[0])
        pieces = (even[:, :256] + even[:, 256:], even[:, :256] - even[:, 256:], odd[:, :256], odd[:, 256:], -odd[:, 256:])
        for k, piece in enumerate(pieces):
            hi, lo = split(piece)
            part_hi[here, 256 * k : 256 * (k + 1)] = hi
            part_lo[here, 256 * k : 256 * (k + 1)] = lo
        if t < LZ:
            for step in range(half * t // LZ, half * (t + 1) // LZ):
                wall_step(step)
    table_copies[0].wait()
    lower, upper, inverse = wall_rows(heights, 256)
    small = sum(shared[512 + k * SMALL : 512 + (k + 1) * SMALL, :].astype(f32) for k in range(3))
    q_first, q_last, mask, mu = (small[16 + k * LY : 16 + (k + 1) * LY] for k in range(4))

    def transform(piece, wave):
        a = (part_hi[:, 256 * piece : 256 * (piece + 1)], part_lo[:, 256 * piece : 256 * (piece + 1)])
        first = 512 * wave
        return dot3(a, (pack[first : first + 256, :], pack[first + 256 : first + 512, :]))

    for i in range(KX):
        if i < 2:
            table_copies[1].wait() if i == 0 else None
            lines = transform(i, i)
        elif i == 2:
            table_copies[2].wait()
            lines = transform(2, 2) + transform(4, 3)
        else:
            lines = transform(2, 3) + transform(3, 2)
        cells = dot3((shared[:256, :], shared[256:512, :]), split(lines[: LZ * LY]))
        crown = dot3((shared[:LY, :LY], shared[256 : 256 + LY, :LY]), split(lines[LZ * LY : (LZ + 1) * LY]))
        edge = lines[(LZ + 1) * LY : (LZ + 1) * LY + LZ]
        kept[i] = cells
        layers = [cells[t * LY : (t + 1) * LY] for t in range(LZ)]
        pivots = block_pivots(mu + small[i : i + 1], mask, lower, upper)
        for t in range(1, LZ):
            block[i, (t - 1) * LY : t * LY, :] = pivots[t]
        inner = block_solve(layers, pivots, lower, upper)
        ends[i * LY : (i + 1) * LY, :] = layers[0] + upper[0] * inner[1]
        ends[128 + i * LY : 128 + (i + 1) * LY, :] = crown + lower[LZ] * inner[LZ - 1]
        own = [jnp.zeros((1, 256), f32)]
        following = [jnp.zeros((1, 256), f32)]
        for t in range(1, LZ):
            own.append(layers[t][:1] + jnp.sum(inner[t] * q_first, axis=0, keepdims=True))
            following.append(jnp.sum(inner[t] * q_last, axis=0, keepdims=True))
        ends[256 + i * LZ : 256 + (i + 1) * LZ, :] = jnp.concatenate(own, axis=0)
        ends[320 + i * LZ : 320 + (i + 1) * LZ, :] = edge + jnp.concatenate(following, axis=0)
    ends[256 + KX * LZ : 320, :] = jnp.zeros((64 - KX * LZ, 256), f32)
    ends[320 + KX * LZ : 384, :] = jnp.zeros((64 - KX * LZ, 256), f32)
    for r in range(3):
        message[pl.ds(r, DEV, stride=3), :] = ends[128 * r : 128 * (r + 1), :].T
    for copy in ahead:
        copy.wait()


def interface(
    arrived, book, slabs, low, up, pivot, reply, value, spec, lines, top, back,
):
    dft_hi, dft_lo, idft = slabs[:128, :], slabs[128:256, :], slabs[256:, :]
    idft_hi, idft_lo = idft[:, :128], idft[:, 128:]
    fwd = lambda k, m: book[pl.ds(LEAF + (k * LY + m) * GY, GY), :]
    inv = lambda k, j: book[pl.ds(LEAF + 2 * LY * GY + (k * GY + j) * LY, LY), :]
    half = NZ // 2
    lane = lax.broadcasted_iota(jnp.int32, (GY, 128), 1)
    field = [arrived[pl.ds(3 * a, GY, stride=3 * GZ), :] for a in range(GZ)]
    for a in range(1, GZ):
        field[a] = field[a] + arrived[pl.ds(3 * (a - 1) + 1, GY, stride=3 * GZ), :]
    for g in range(2):
        blocks = []
        for i in range(KX):
            block = None
            for k in range(4):
                moved = pltpu.roll(field[4 * g + k], (32 * (k - i)) % 128, axis=1)
                block = moved if block is None else jnp.where(lane // 32 == k, moved, block)
            blocks.append(block)
        stacked = jnp.concatenate(blocks, axis=0).T
        spec[128 * g : 128 * (g + 1), :] = dot3(split(stacked), (dft_hi, dft_lo))
    sides = []
    for a in range(GZ):
        rest = arrived[pl.ds(3 * a + 2, GY, stride=3 * GZ), :]
        sides.append(rest + pltpu.roll(pltpu.roll(rest, 64, axis=1), 1, axis=0))
    blocks = []
    for i in range(KX):
        block = jnp.zeros((GY, 128), f32)
        for a in range(GZ):
            moved = pltpu.roll(sides[a], (8 * (a - i)) % 128, axis=1)
            block = jnp.where(lane // 8 == a, moved, block)
        blocks.append(block)
    stacked = jnp.concatenate(blocks, axis=0).T[:NZ]
    lines[...] = dot3(split(stacked), (dft_hi[:, :128], dft_lo[:, :128]))
    for g in range(2):
        total = [jnp.zeros((GY, 128), f32)] * 4
        for m in range(LY):
            c_main = fwd(0, m)
            c_partner = fwd(1, m)
            for k in range(4):
                row = 128 * g + 32 * k + m
                total[k] = total[k] + c_main * spec[row : row + 1, :128] + c_partner * spec[row : row + 1, 128:]
        for k in range(4):
            top[4 * g + k] = total[k]
    weight = fwd(0, 0)
    for s in range(half):
        for z in (s, NZ - 1 - s):
            right = weight * lines[z : z + 1, :]
            if z % LZ == 0:
                right = right + top[z // LZ]
            if s > 0:
                if z < half:
                    right = right + low[z : z + 1, :] * value[z - 1]
                else:
                    right = right + up[z : z + 1, :] * value[z + 1]
            value[z] = right * pivot[z]
    alpha = up[half - 1 : half, :] * pivot[half - 1]
    beta = low[half : half + 1, :] * pivot[half]
    below = (value[half - 1] + alpha * value[half]) / (1.0 - alpha * beta)
    above = value[half] + beta * below
    for s in range(half):
        for z in (half - 1 - s, half + s):
            if z < half:
                if s > 0:
                    below = value[z] + up[z : z + 1, :] * pivot[z] * below
                now = below
            else:
                if s > 0:
                    above = value[z] + low[z : z + 1, :] * pivot[z] * above
                now = above
            lines[z : z + 1, :] = jnp.sum(now * weight, axis=0, keepdims=True)
            if z % LZ == 0:
                top[z // LZ] = now
    for g in range(2):
        total = [jnp.zeros((LY, 128), f32)] * 4
        other = [jnp.zeros((LY, 128), f32)] * 4
        for j in range(GY):
            c_main = inv(0, j)
            c_partner = inv(1, j)
            for k in range(4):
                row = top[4 * g + k, j : j + 1, :]
                total[k] = total[k] + c_main * row
                other[k] = other[k] + c_partner * row
        for k in range(4):
            spec[128 * g + 32 * k : 128 * g + 32 * (k + 1), :128] = total[k]
            spec[128 * g + 32 * k : 128 * g + 32 * (k + 1), 128:] = other[k]
    for g in range(2):
        back[...] = dot3(split(spec[128 * g : 128 * (g + 1), :]), (idft_hi, idft_lo)).T
        for k in range(4):
            block = None
            for i in range(KX):
                moved = pltpu.roll(back[32 * i : 32 * (i + 1), :], (32 * (i - k)) % 128, axis=1)
                block = moved if block is None else jnp.where(lane // 32 == i, moved, block)
            a = 4 * g + k
            reply[pl.ds(3 * a, GY, stride=3 * GZ), :] = block
            if a > 0:
                reply[pl.ds(3 * (a - 1) + 1, GY, stride=3 * GZ), :] = block
    reply[pl.ds(3 * (GZ - 1) + 1, GY, stride=3 * GZ), :] = jnp.zeros((GY, 128), f32)
    rest = dot3(split(lines[...]), (idft_hi[:128, :], idft_lo[:128, :]))
    back[...] = jnp.concatenate([rest, rest], axis=0).T
    pieces = []
    for i in range(KX):
        piece = back[32 * i : 32 * (i + 1), :]
        pieces.append(jnp.where(lane < 64, piece, pltpu.roll(piece, GY - 1, axis=0)))
    for a in range(GZ):
        block = jnp.zeros((GY, 128), f32)
        for i in range(KX):
            moved = pltpu.roll(pieces[i], (8 * (i - a)) % 128, axis=1)
            block = jnp.where((lane % 64) // 8 == i, moved, block)
        reply[pl.ds(3 * a + 2, GY, stride=3 * GZ), :] = block


def restore(
    rows, arrived, kept, shared, block, pack, pressure, ends, result, out_sem,
):
    lower, upper, _ = wall_rows(rows, 256)
    small = sum(shared[512 + k * SMALL : 512 + (k + 1) * SMALL, :].astype(f32) for k in range(3))
    q_first, q_last, mask = (small[16 + k * LY : 16 + (k + 1) * LY] for k in range(3))
    for r in range(3):
        ends[128 * r : 128 * (r + 1), :] = arrived[pl.ds(r, DEV, stride=3), :].T
    lines = []
    for i in range(KX):
        floor = ends[i * LY : (i + 1) * LY, :]
        ceiling = ends[128 + i * LY : 128 + (i + 1) * LY, :]
        pivots = [None] + [block[i, (t - 1) * LY : t * LY, :] for t in range(1, LZ)]
        right = [None] * LZ
        near = [None] * LZ
        for t in range(1, LZ):
            near[t] = ends[256 + i * LZ + t : 256 + i * LZ + t + 1, :]
            far = ends[320 + i * LZ + t : 320 + i * LZ + t + 1, :]
            right[t] = kept[i, t * LY : (t + 1) * LY, :] + (q_first * near[t] + q_last * far)
        right[1] = right[1] + lower[1] * floor
        right[LZ - 1] = right[LZ - 1] + upper[LZ - 1] * ceiling
        inner = block_solve(right, pivots, lower, upper)
        layers = [floor] + [inner[t] + (1.0 - mask) * near[t] for t in range(1, LZ)]
        modes = jnp.concatenate(layers, axis=0)
        lines.append(dot3((shared[:256, :], shared[256:512, :]), split(modes)))

    def transform(line, wave):
        first = 512 * wave
        return dot3(line, (pack[first : first + 256, :], pack[first + 256 : first + 512, :]))

    minus = split(-lines[2])
    lines = [split(line) for line in lines]
    even = transform(lines[0], 0)
    odd = transform(lines[1], 1)
    copies = []
    for q in range(2):
        if q == 0:
            whole = even + odd
            swing = transform(lines[2], 2) + transform(lines[3], 3)
        else:
            whole = even - odd
            swing = transform(minus, 3) + transform(lines[3], 2)
        for k, piece in ((q, whole + swing), (q + 2, whole - swing)):
            here = pl.ds(256 * k, 256)
            result[:, :, 256 * k : 256 * (k + 1)] = piece.reshape(LZ, LY, 256)
            copy = pltpu.make_async_copy(result.at[:, :, here], pressure.at[:, :, here], out_sem.at[k])
            copy.start()
            copies.append(copy)
    for copy in copies:
        copy.wait()


def on_device(streamwise, spanwise, wall_normal, spacing):
    far = lambda x: pltpu.with_memory_space_constraint(x, pltpu.HBM)
    near = lambda x: pltpu.with_memory_space_constraint(x, pltpu.VMEM)
    pack, book, later = (jnp.asarray(part) for part in tables())
    pack, book = far(pack), far(book)
    vmem = pl.BlockSpec(memory_space=pltpu.VMEM)
    hbm = pl.BlockSpec(memory_space=pltpu.HBM)
    params = pltpu.CompilerParams(vmem_limit_bytes=50 * 2**20)
    shape = jax.ShapeDtypeStruct
    message, kept, heights, book, slabs, low, up, pivot, block, shared = pl.pallas_call(
        eliminate,
        out_shape=(
            pltpu.VMEM((3 * DEV, 128), f32),
            pltpu.VMEM((KX, LZ * LY, 256), f32),
            pltpu.VMEM((NZ, 128), f32),
            pltpu.VMEM((BOOK, 128), f32),
            pltpu.VMEM((512, 256), bf16),
            pltpu.VMEM((NZ, 128), f32),
            pltpu.VMEM((NZ, 128), f32),
            pltpu.VMEM((NZ, GY, 128), f32),
            pltpu.VMEM((KX, (LZ - 1) * LY, 256), f32),
            pltpu.VMEM((SHARED, 256), bf16),
        ),
        in_specs=[hbm] * 6,
        out_specs=(vmem,) * 10,
        scratch_shapes=[
            pltpu.SMEM((NZ,), f32),
            pltpu.VMEM((LZ, LY, NX), f32),
            pltpu.VMEM((LZ, LY, NX), f32),
            pltpu.VMEM((LZ, LY, NX), f32),
            pltpu.VMEM((8 * 256, 256), bf16),
            pltpu.VMEM(((LZ + 1) * LY + 16, NX + 256), bf16),
            pltpu.VMEM(((LZ + 1) * LY + 16, NX + 256), bf16),
            pltpu.VMEM((384, 256), f32),
            pltpu.SemaphoreType.DMA((LZ // 2, 3)),
            pltpu.SemaphoreType.DMA((7,)),
        ],
        compiler_params=params,
        name="eliminate",
    )(far(spacing), far(streamwise), far(spanwise), far(wall_normal), pack, book)
    axes = ("gy", "gz")
    trade = lambda x: lax.all_to_all(
        x.reshape(DEV, 1, 384), axes, split_axis=0, concat_axis=0, tiled=True
    ).reshape(3 * DEV, 128)
    arrived = trade(message)
    reply = pl.pallas_call(
        interface,
        out_shape=pltpu.VMEM((3 * DEV, 128), f32),
        in_specs=[vmem] * 6,
        out_specs=vmem,
        scratch_shapes=[
            pltpu.VMEM((NZ, GY, 128), f32),
            pltpu.VMEM((256, 256), f32),
            pltpu.VMEM((NZ, 128), f32),
            pltpu.VMEM((GZ, GY, 128), f32),
            pltpu.VMEM((128, 128), f32),
        ],
        compiler_params=params,
        name="interface",
    )(near(arrived), near(book), near(slabs), near(low), near(up), near(pivot))
    answered = trade(reply)
    return pl.pallas_call(
        restore,
        out_shape=shape((LZ, LY, NX), f32),
        in_specs=[vmem] * 6,
        out_specs=hbm,
        scratch_shapes=[
            pltpu.VMEM((384, 256), f32),
            pltpu.VMEM((LZ, LY, NX), f32),
            pltpu.SemaphoreType.DMA((4,)),
        ],
        compiler_params=params,
        name="restore",
    )(near(heights), near(answered), near(kept), near(shared), near(block), near(later))


def solution(mesh):
    placed = (P("gz", "gy", None), P("gz", "gy", None), P("gz", "gy", None), P())
    return jax.shard_map(
        on_device, mesh=mesh, in_specs=placed, out_specs=P("gz", "gy", None), check_vma=False
    )
```

```python
import functools
import math

import jax
import jax.numpy as jnp
import ml_dtypes
import numpy as np
from jax import lax
from jax.experimental import pallas as pl
from jax.experimental.pallas import tpu as pltpu
from jax.sharding import PartitionSpec as P

screening = 0.0015
NX = 1024
NY = 1024
NZ = 64
GZ = 8
GY = 32
LZ = NZ // GZ
LY = NY // GY
DEV = GZ * GY
KX = NX // DEV
SMALL = 144
SHARED = 512 + 3 * SMALL
FORWARD = SHARED + 8 * 256
BACKWARD = FORWARD + 8 * 256
SLABS = BACKWARD + 512
LEAF = GY + DEV
EARLY = 6
HALF = EARLY * LY
ROWS = (HALF, (LZ + 1) * LY - HALF + 16)
BOOK = LEAF + 4 * GY * LY
f32 = jnp.float32
bf16 = jnp.bfloat16


def basis(count):
    j = np.arange(count)[:, None]
    m = np.arange(count)[None, :]
    half = count // 2
    wave = np.where(m <= half, m, m - half)
    angle = 2.0 * np.pi / count * ((j * wave) % count)
    scale = np.where((m == 0) | (m == half), 1.0, math.sqrt(2.0)) / math.sqrt(count)
    return np.where(m <= half, np.cos(angle), np.sin(angle)) * scale


def eigen(count):
    m = np.arange(count)
    half = count // 2
    wave = np.where(m <= half, m, m - half)
    return 2.0 - 2.0 * np.cos(2.0 * np.pi / count * wave)


def two(x):
    hi = np.asarray(x, np.float64).astype(ml_dtypes.bfloat16)
    lo = (x - hi.astype(np.float64)).astype(ml_dtypes.bfloat16)
    return hi, lo


@functools.lru_cache(maxsize=None)
def tables():
    half = NX // 2
    tx = basis(NX)
    ex = eigen(NX)
    columns = [
        np.concatenate([np.arange(0, half + 1, 4), half + np.arange(4, half, 4)]),
        np.concatenate([np.arange(2, half, 4), half + np.arange(2, half, 4)]),
    ]
    quarter = np.arange(256)
    turn = 2.0 * np.pi / NX * (quarter[:, None] * (4 * quarter[None, :] + 1) % NX)
    waves = math.sqrt(2.0 / NX) * np.cos(turn), math.sqrt(2.0 / NX) * np.sin(turn)
    parts = [tx[:256, columns[0]], tx[:256, columns[1]], *waves]
    lam_odd = 2.0 - 2.0 * np.cos(2.0 * np.pi / NX * (4 * quarter + 1))
    lam_x = np.stack([ex[columns[0]], ex[columns[1]], lam_odd, lam_odd])

    sine = np.zeros((LY, LY))
    sine[0, 0] = 1.0
    m = np.arange(1, LY)
    sine[1:, 1:] = math.sqrt(2.0 / LY) * np.sin(np.pi * m[:, None] * m[None, :] / LY)
    mu = np.full((LY,), 2.0)
    mu[1:] = 2.0 - 2.0 * np.cos(np.pi * m / LY)
    kron = np.kron(np.eye(LZ), sine)
    q_first = sine[:, 1].copy()
    q_first[0] = 0.0
    q_last = sine[:, LY - 1].copy()
    q_last[0] = 0.0
    mask = np.ones((LY,))
    mask[0] = 0.0
    side = np.stack([np.repeat(v[:, None], 256, axis=1) for v in (q_first, q_last, mask)])
    small = np.zeros((SMALL, 256))
    small[:KX] = lam_x
    small[16 : 16 + 3 * LY] = side.reshape(3 * LY, 256)
    small[16 + 3 * LY :] = mu[:, None] + screening
    rest, thirds = small.astype(np.float32).astype(np.float64), []
    for _ in range(3):
        thirds.append(rest.astype(ml_dtypes.bfloat16))
        rest = rest - thirds[-1].astype(np.float64)
    pack = [*two(kron), *thirds]
    for part in parts:
        pack += two(part)
    for part in parts:
        pack += two(part.T)

    ty = basis(NY)
    ey = eigen(NY)
    main = basis(GY)
    partner = np.zeros((GY, GY))
    for p in range(1, GY // 2):
        partner[:, p] = main[:, GY // 2 + p]
        partner[:, GY // 2 + p] = main[:, p]
    wave = np.where(np.arange(NY) <= NY // 2, np.arange(NY), np.arange(NY) - NY // 2)
    is_cos = np.arange(NY) <= NY // 2
    fold = wave % GY
    fold = np.minimum(fold, GY - fold)
    order = np.zeros((GY, GY), np.int64)
    for p in range(GY):
        if p in (0, GY // 2):
            order[:, p] = np.nonzero(fold == p)[0]
        elif p < GY // 2:
            order[:, p] = np.nonzero((fold == p) & is_cos)[0]
        else:
            order[:, p] = np.nonzero((fold == p - GY // 2) & ~is_cos)[0]
    shaped = ty.reshape(GY, LY, NY)[:, :, order]
    a_y = np.einsum("bvjp,bp->vjp", shaped, main)
    b_y = np.einsum("bvjp,bp->vjp", shaped, partner)
    a_m = np.einsum("mv,vjp->mjp", sine, a_y)
    b_m = np.einsum("mv,vjp->mjp", sine, b_y)
    a_m = np.tile(a_m, (1, 1, KX))
    b_m = np.tile(b_m, (1, 1, KX))
    lam_y = np.tile(ey[order], (1, KX)) + screening
    lam_d = np.repeat(lam_x.T, GY, axis=1)
    spread = np.eye(KX)
    dft = np.concatenate([np.kron(spread, main), np.kron(spread, partner)], axis=1)
    pack += two(dft)
    pack.append(np.concatenate(two(dft.T), axis=1))
    pack = np.concatenate(pack, axis=0)
    assert pack.shape == (SLABS, 256)
    later = pack[FORWARD:BACKWARD]
    both = np.stack([a_m, b_m])
    book = [lam_y, lam_d, both, both.transpose(0, 2, 1, 3)]
    book = np.concatenate([part.reshape(-1, 128) for part in book], axis=0).astype(np.float32)
    assert book.shape == (BOOK, 128)
    return pack, book, later


def split(x):
    hi = x.astype(bf16)
    return hi, (x - hi.astype(f32)).astype(bf16)


def dot(a, b):
    return lax.dot_general(a, b, (((1,), (0,)), ((), ())), preferred_element_type=f32)


def dot3(a, b):
    return dot(a[0], b[0]) + (dot(a[0], b[1]) + dot(a[1], b[0]))


def stacked3(a, count, high, low):
    full = dot(a, high)
    return full[:count] + (full[count:] + dot(a[:count], low))


def sandwich(kron, lines):
    hi, lo = split(lines)
    full = dot(kron, hi)
    count = lines.shape[0]
    return full[:count] + (full[count:] + dot(kron[:count], lo))


def wall_rows(rows, width):
    first = lax.axis_index("gz") * LZ
    inside = first + LZ < NZ
    places = [first + t for t in range(LZ)] + [jnp.minimum(first + LZ, NZ - 1)]
    heights = [jnp.concatenate([rows[pl.ds(place, 1), :]] * (width // 128), axis=1) for place in places]
    gaps = [0.5 * (heights[t] + heights[t + 1]) for t in range(LZ)]
    keep = jnp.where(inside, 1.0, 0.0).astype(f32)
    lower = [None] + [1.0 / (gaps[t - 1] * heights[t]) for t in range(1, LZ + 1)]
    upper = [1.0 / (gaps[t] * heights[t]) for t in range(LZ)]
    inverse = [1.0 / heights[t] for t in range(LZ + 1)]
    lower[LZ] = lower[LZ] * keep
    upper[LZ - 1] = upper[LZ - 1] * keep
    inverse[LZ] = inverse[LZ] * keep
    return lower, upper, inverse


def block_pivots(off, mask, lower, upper):
    pivots = [None] * LZ
    for t in range(1, LZ):
        diagonal = off + (lower[t] + upper[t])
        if t > 1:
            diagonal = diagonal - (lower[t] * upper[t - 1]) * pivots[t - 1]
        pivots[t] = mask / diagonal
    return pivots


def block_solve(right, pivots, lower, upper):
    value = [None] * LZ
    for t in range(1, LZ):
        term = right[t] if t == 1 else right[t] + lower[t] * value[t - 1]
        value[t] = term * pivots[t]
    for t in range(LZ - 2, 0, -1):
        value[t] = value[t] + upper[t] * pivots[t] * value[t + 1]
    return value


def eliminate(
    spacing_in, stream_in, span_in, wall_in, pack_in, book_in,
    message, kept, heights, book, slabs, low, up, pivot, block, shared,
    spacing, stream, span, wall, pack, part_0, part_1, part_2, part_3, part_4, part_5, ends, cell_sem, table_sem,
):
    first_copy = pltpu.make_async_copy(spacing_in, spacing, table_sem.at[0])
    first_copy.start()
    leaf = pltpu.make_async_copy(book_in.at[pl.ds(0, LEAF)], book.at[pl.ds(0, LEAF)], table_sem.at[4])
    leaf.start()
    copies = []
    for t in range(0, LZ, 2):
        here = pl.ds(t, 2)
        trio = [
            pltpu.make_async_copy(source.at[here], target.at[here], cell_sem.at[t // 2, k])
            for k, (source, target) in enumerate(((stream_in, stream), (span_in, span), (wall_in, wall)))
        ]
        for copy in trio:
            copy.start()
        copies.append(trio)
        if t == 2:
            table_copies = []
            moves = (
                (pack_in.at[pl.ds(0, SHARED)], shared),
                (pack_in.at[pl.ds(SHARED, 1024)], pack.at[pl.ds(0, 1024)]),
                (pack_in.at[pl.ds(SHARED + 1024, 1024)], pack.at[pl.ds(1024, 1024)]),
            )
            for k, (source, target) in enumerate(moves):
                table_copies.append(pltpu.make_async_copy(source, target, table_sem.at[k + 1]))
                table_copies[-1].start()
    ahead = [
        pltpu.make_async_copy(pack_in.at[pl.ds(BACKWARD, 512)], slabs, table_sem.at[5]),
        pltpu.make_async_copy(
            book_in.at[pl.ds(LEAF, BOOK - LEAF)], book.at[pl.ds(LEAF, BOOK - LEAF)], table_sem.at[6]
        ),
    ]
    for copy in ahead:
        copy.start()
    first_copy.wait()
    for z in range(NZ):
        heights[z : z + 1, :] = jnp.full((1, 128), spacing[z], f32)
    tall = heights[...]
    layer = lax.broadcasted_iota(jnp.int32, (NZ, 128), 0)
    gap = 0.5 * (tall + pltpu.roll(tall, NZ - 1, axis=0))
    low[...] = jnp.where(layer == 0, 0.0, 1.0 / (pltpu.roll(gap, 1, axis=0) * tall))
    up[...] = jnp.where(layer == NZ - 1, 0.0, 1.0 / (gap * tall))
    leaf.wait()
    me = lax.axis_index("gy") * GZ + lax.axis_index("gz")
    off = book[pl.ds(0, GY), :] + book[pl.ds(GY + me, 1), :]
    half = NZ // 2
    last = [None, None]

    def wall_step(s):
        for side, z in enumerate((s, NZ - 1 - s)):
            diagonal = off + (low[z : z + 1, :] + up[z : z + 1, :])
            if s > 0 and side == 0:
                diagonal = diagonal - (low[z : z + 1, :] * up[z - 1 : z, :]) * last[0]
            if s > 0 and side == 1:
                diagonal = diagonal - (up[z : z + 1, :] * low[z + 1 : z + 2, :]) * last[1]
            last[side] = 1.0 / diagonal
            pivot[z] = last[side]

    lower, upper, inverse = wall_rows(heights, NX)
    rows = lax.broadcasted_iota(jnp.int32, (LY, NX), 0)
    extra = []

    def transform(part, wave):
        first = 512 * wave
        return stacked3(part[...], part.shape[0] // 2, pack[first : first + 256, :], pack[first + 256 : first + 512, :])

    def transform_group(parts, group):
        count = ROWS[group]
        lines = [transform(parts[0], 0), transform(parts[1], 1)]
        cosine, sine = transform(parts[2], 2), transform(parts[2], 3)
        lines += [cosine[:count] - sine[count:], sine[:count] + cosine[count:]]
        size = (HALF, LZ * LY - HALF)[group]
        sines = shared[:size, :size], shared[256 : 256 + size, :size]
        for i in range(KX):
            kept[i, group * HALF : group * HALF + size, :] = dot3(sines, split(lines[i][:size]))
            if group == 1:
                crown = dot3((sines[0][:LY, :LY], sines[1][:LY, :LY]), split(lines[i][size : size + LY]))
                extra.append((crown, lines[i][size + LY : size + LY + LZ]))

    for t in range(LZ + 2):
        if t < LZ:
            if t % 2 == 0:
                for copy in copies[t // 2]:
                    copy.wait()
            u = stream[t]
            v = span[t]
            w = wall[t]
            shifted = jnp.where(rows == 0, 0.0, pltpu.roll(v, 1, axis=0))
            d = (pltpu.roll(u, 1, axis=1) - u) + (shifted - v)
            d = d - w * inverse[t] if t == 0 else d + (wall[t - 1] - w) * inverse[t]
        elif t == LZ:
            d = wall[LZ - 1] * inverse[LZ]
        else:
            d = jnp.concatenate([span[z, LY - 1 :, :] for z in range(LZ)] + [jnp.zeros((8, NX), f32)], axis=0)
        even = d[:, :512] + d[:, 512:]
        odd = d[:, :512] - d[:, 512:]
        pieces = (even[:, :256] + even[:, 256:], even[:, :256] - even[:, 256:], odd[:, :256], odd[:, 256:])
        for k, piece in enumerate(pieces):
            hi, lo = split(piece)
            group = 0 if t < EARLY else 1
            count = ROWS[group]
            parts = ((part_0, part_1, part_2, part_2), (part_3, part_4, part_5, part_5))[group]
            for part, level in ((hi, 0), (lo, 1)):
                first = (level, level, 2 * level, 2 * level + 1)[k] * count + t * LY - group * HALF
                parts[k][first : first + d.shape[0], :] = part
        if t < LZ:
            for step in range(half * t // LZ, half * (t + 1) // LZ):
                wall_step(step)
        if t == EARLY - 1:
            for copy in table_copies:
                copy.wait()
            transform_group((part_0, part_1, part_2), 0)
    transform_group((part_3, part_4, part_5), 1)
    lower, upper, inverse = wall_rows(heights, 256)
    small = sum(shared[512 + k * SMALL : 512 + (k + 1) * SMALL, :].astype(f32) for k in range(3))
    q_first, q_last, mask, mu = (small[16 + k * LY : 16 + (k + 1) * LY] for k in range(4))
    for i in range(KX):
        cells = kept[i]
        crown, edge = extra[i]
        layers = [cells[t * LY : (t + 1) * LY] for t in range(LZ)]
        pivots = block_pivots(mu + small[i : i + 1], mask, lower, upper)
        for t in range(1, LZ):
            block[i, (t - 1) * LY : t * LY, :] = pivots[t]
        inner = block_solve(layers, pivots, lower, upper)
        ends[i * LY : (i + 1) * LY, :] = layers[0] + upper[0] * inner[1]
        ends[128 + i * LY : 128 + (i + 1) * LY, :] = crown + lower[LZ] * inner[LZ - 1]
        own = [jnp.zeros((1, 256), f32)]
        following = [jnp.zeros((1, 256), f32)]
        for t in range(1, LZ):
            own.append(layers[t][:1] + jnp.sum(inner[t] * q_first, axis=0, keepdims=True))
            following.append(jnp.sum(inner[t] * q_last, axis=0, keepdims=True))
        ends[256 + i * LZ : 256 + (i + 1) * LZ, :] = jnp.concatenate(own, axis=0)
        ends[320 + i * LZ : 320 + (i + 1) * LZ, :] = edge + jnp.concatenate(following, axis=0)
    ends[256 + KX * LZ : 320, :] = jnp.zeros((64 - KX * LZ, 256), f32)
    ends[320 + KX * LZ : 384, :] = jnp.zeros((64 - KX * LZ, 256), f32)
    for r in range(3):
        message[pl.ds(r, DEV, stride=3), :] = ends[128 * r : 128 * (r + 1), :].T
    for copy in ahead:
        copy.wait()


def interface(
    arrived, book, slabs, low, up, pivot, reply, value, spec, lines, top, back,
):
    dft_hi, dft_lo, idft = slabs[:128, :], slabs[128:256, :], slabs[256:, :]
    idft_hi, idft_lo = idft[:, :128], idft[:, 128:]
    fwd = lambda k, m: book[pl.ds(LEAF + (k * LY + m) * GY, GY), :]
    inv = lambda k, j: book[pl.ds(LEAF + 2 * LY * GY + (k * GY + j) * LY, LY), :]
    half = NZ // 2
    lane = lax.broadcasted_iota(jnp.int32, (GY, 128), 1)
    field = [arrived[pl.ds(3 * a, GY, stride=3 * GZ), :] for a in range(GZ)]
    for a in range(1, GZ):
        field[a] = field[a] + arrived[pl.ds(3 * (a - 1) + 1, GY, stride=3 * GZ), :]
    for g in range(2):
        blocks = []
        for i in range(KX):
            block = None
            for k in range(4):
                moved = pltpu.roll(field[4 * g + k], (32 * (k - i)) % 128, axis=1)
                block = moved if block is None else jnp.where(lane // 32 == k, moved, block)
            blocks.append(block)
        stacked = jnp.concatenate(blocks, axis=0).T
        spec[128 * g : 128 * (g + 1), :] = dot3(split(stacked), (dft_hi, dft_lo))
    sides = []
    for a in range(GZ):
        rest = arrived[pl.ds(3 * a + 2, GY, stride=3 * GZ), :]
        sides.append(rest + pltpu.roll(pltpu.roll(rest, 64, axis=1), 1, axis=0))
    blocks = []
    for i in range(KX):
        block = jnp.zeros((GY, 128), f32)
        for a in range(GZ):
            moved = pltpu.roll(sides[a], (8 * (a - i)) % 128, axis=1)
            block = jnp.where(lane // 8 == a, moved, block)
        blocks.append(block)
    stacked = jnp.concatenate(blocks, axis=0).T[:NZ]
    lines[...] = dot3(split(stacked), (dft_hi[:, :128], dft_lo[:, :128]))
    for g in range(2):
        total = [jnp.zeros((GY, 128), f32)] * 4
        for m in range(LY):
            c_main = fwd(0, m)
            c_partner = fwd(1, m)
            for k in range(4):
                row = 128 * g + 32 * k + m
                total[k] = total[k] + c_main * spec[row : row + 1, :128] + c_partner * spec[row : row + 1, 128:]
        for k in range(4):
            top[4 * g + k] = total[k]
    weight = fwd(0, 0)
    for s in range(half):
        for z in (s, NZ - 1 - s):
            right = weight * lines[z : z + 1, :]
            if z % LZ == 0:
                right = right + top[z // LZ]
            if s > 0:
                if z < half:
                    right = right + low[z : z + 1, :] * value[z - 1]
                else:
                    right = right + up[z : z + 1, :] * value[z + 1]
            value[z] = right * pivot[z]
    alpha = up[half - 1 : half, :] * pivot[half - 1]
    beta = low[half : half + 1, :] * pivot[half]
    below = (value[half - 1] + alpha * value[half]) / (1.0 - alpha * beta)
    above = value[half] + beta * below
    for s in range(half):
        for z in (half - 1 - s, half + s):
            if z < half:
                if s > 0:
                    below = value[z] + up[z : z + 1, :] * pivot[z] * below
                now = below
            else:
                if s > 0:
                    above = value[z] + low[z : z + 1, :] * pivot[z] * above
                now = above
            lines[z : z + 1, :] = jnp.sum(now * weight, axis=0, keepdims=True)
            if z % LZ == 0:
                top[z // LZ] = now
    for g in range(2):
        total = [jnp.zeros((LY, 128), f32)] * 4
        other = [jnp.zeros((LY, 128), f32)] * 4
        for j in range(GY):
            c_main = inv(0, j)
            c_partner = inv(1, j)
            for k in range(4):
                row = top[4 * g + k, j : j + 1, :]
                total[k] = total[k] + c_main * row
                other[k] = other[k] + c_partner * row
        for k in range(4):
            spec[128 * g + 32 * k : 128 * g + 32 * (k + 1), :128] = total[k]
            spec[128 * g + 32 * k : 128 * g + 32 * (k + 1), 128:] = other[k]
    for g in range(2):
        back[...] = dot3(split(spec[128 * g : 128 * (g + 1), :]), (idft_hi, idft_lo)).T
        for k in range(4):
            block = None
            for i in range(KX):
                moved = pltpu.roll(back[32 * i : 32 * (i + 1), :], (32 * (i - k)) % 128, axis=1)
                block = moved if block is None else jnp.where(lane // 32 == i, moved, block)
            a = 4 * g + k
            reply[pl.ds(3 * a, GY, stride=3 * GZ), :] = block
            if a > 0:
                reply[pl.ds(3 * (a - 1) + 1, GY, stride=3 * GZ), :] = block
    reply[pl.ds(3 * (GZ - 1) + 1, GY, stride=3 * GZ), :] = jnp.zeros((GY, 128), f32)
    rest = dot3(split(lines[...]), (idft_hi[:128, :], idft_lo[:128, :]))
    back[...] = jnp.concatenate([rest, rest], axis=0).T
    pieces = []
    for i in range(KX):
        piece = back[32 * i : 32 * (i + 1), :]
        pieces.append(jnp.where(lane < 64, piece, pltpu.roll(piece, GY - 1, axis=0)))
    for a in range(GZ):
        block = jnp.zeros((GY, 128), f32)
        for i in range(KX):
            moved = pltpu.roll(pieces[i], (8 * (i - a)) % 128, axis=1)
            block = jnp.where((lane % 64) // 8 == i, moved, block)
        reply[pl.ds(3 * a + 2, GY, stride=3 * GZ), :] = block


def restore(
    rows, arrived, kept, shared, block, pack, pressure, ends, result, out_sem,
):
    lower, upper, _ = wall_rows(rows, 256)
    small = sum(shared[512 + k * SMALL : 512 + (k + 1) * SMALL, :].astype(f32) for k in range(3))
    q_first, q_last, mask = (small[16 + k * LY : 16 + (k + 1) * LY] for k in range(3))
    for r in range(3):
        ends[128 * r : 128 * (r + 1), :] = arrived[pl.ds(r, DEV, stride=3), :].T
    lines = []
    for i in range(KX):
        floor = ends[i * LY : (i + 1) * LY, :]
        ceiling = ends[128 + i * LY : 128 + (i + 1) * LY, :]
        pivots = [None] + [block[i, (t - 1) * LY : t * LY, :] for t in range(1, LZ)]
        right = [None] * LZ
        near = [None] * LZ
        for t in range(1, LZ):
            near[t] = ends[256 + i * LZ + t : 256 + i * LZ + t + 1, :]
            far = ends[320 + i * LZ + t : 320 + i * LZ + t + 1, :]
            right[t] = kept[i, t * LY : (t + 1) * LY, :] + (q_first * near[t] + q_last * far)
        right[1] = right[1] + lower[1] * floor
        right[LZ - 1] = right[LZ - 1] + upper[LZ - 1] * ceiling
        inner = block_solve(right, pivots, lower, upper)
        layers = [floor] + [inner[t] + (1.0 - mask) * near[t] for t in range(1, LZ)]
        modes = jnp.concatenate(layers, axis=0)
        lines.append(sandwich(shared[:512, :], modes))

    def transform(line, wave):
        first = 512 * wave
        return dot3(line, (pack[first : first + 256, :], pack[first + 256 : first + 512, :]))

    minus = split(-lines[2])
    lines = [split(line) for line in lines]
    even = transform(lines[0], 0)
    odd = transform(lines[1], 1)
    copies = []
    for q in range(2):
        if q == 0:
            whole = even + odd
            swing = transform(lines[2], 2) + transform(lines[3], 3)
        else:
            whole = even - odd
            swing = transform(minus, 3) + transform(lines[3], 2)
        for k, piece in ((q, whole + swing), (q + 2, whole - swing)):
            here = pl.ds(256 * k, 256)
            result[:, :, 256 * k : 256 * (k + 1)] = piece.reshape(LZ, LY, 256)
            copy = pltpu.make_async_copy(result.at[:, :, here], pressure.at[:, :, here], out_sem.at[k])
            copy.start()
            copies.append(copy)
    for copy in copies:
        copy.wait()


def on_device(streamwise, spanwise, wall_normal, spacing):
    far = lambda x: pltpu.with_memory_space_constraint(x, pltpu.HBM)
    near = lambda x: pltpu.with_memory_space_constraint(x, pltpu.VMEM)
    pack, book, later = (jnp.asarray(part) for part in tables())
    pack, book = far(pack), far(book)
    vmem = pl.BlockSpec(memory_space=pltpu.VMEM)
    hbm = pl.BlockSpec(memory_space=pltpu.HBM)
    params = pltpu.CompilerParams(vmem_limit_bytes=50 * 2**20)
    shape = jax.ShapeDtypeStruct
    message, kept, heights, book, slabs, low, up, pivot, block, shared = pl.pallas_call(
        eliminate,
        out_shape=(
            pltpu.VMEM((3 * DEV, 128), f32),
            pltpu.VMEM((KX, LZ * LY, 256), f32),
            pltpu.VMEM((NZ, 128), f32),
            pltpu.VMEM((BOOK, 128), f32),
            pltpu.VMEM((512, 256), bf16),
            pltpu.VMEM((NZ, 128), f32),
            pltpu.VMEM((NZ, 128), f32),
            pltpu.VMEM((NZ, GY, 128), f32),
            pltpu.VMEM((KX, (LZ - 1) * LY, 256), f32),
            pltpu.VMEM((SHARED, 256), bf16),
        ),
        in_specs=[hbm] * 6,
        out_specs=(vmem,) * 10,
        scratch_shapes=[
            pltpu.SMEM((NZ,), f32),
            pltpu.VMEM((LZ, LY, NX), f32),
            pltpu.VMEM((LZ, LY, NX), f32),
            pltpu.VMEM((LZ, LY, NX), f32),
            pltpu.VMEM((8 * 256, 256), bf16),
            pltpu.VMEM((2 * ROWS[0], 256), bf16),
            pltpu.VMEM((2 * ROWS[0], 256), bf16),
            pltpu.VMEM((4 * ROWS[0], 256), bf16),
            pltpu.VMEM((2 * ROWS[1], 256), bf16),
            pltpu.VMEM((2 * ROWS[1], 256), bf16),
            pltpu.VMEM((4 * ROWS[1], 256), bf16),
            pltpu.VMEM((384, 256), f32),
            pltpu.SemaphoreType.DMA((LZ // 2, 3)),
            pltpu.SemaphoreType.DMA((7,)),
        ],
        compiler_params=params,
        name="eliminate",
    )(far(spacing), far(streamwise), far(spanwise), far(wall_normal), pack, book)
    axes = ("gy", "gz")
    trade = lambda x: lax.all_to_all(
        x.reshape(DEV, 1, 384), axes, split_axis=0, concat_axis=0, tiled=True
    ).reshape(3 * DEV, 128)
    arrived = trade(message)
    reply = pl.pallas_call(
        interface,
        out_shape=pltpu.VMEM((3 * DEV, 128), f32),
        in_specs=[vmem] * 6,
        out_specs=vmem,
        scratch_shapes=[
            pltpu.VMEM((NZ, GY, 128), f32),
            pltpu.VMEM((256, 256), f32),
            pltpu.VMEM((NZ, 128), f32),
            pltpu.VMEM((GZ, GY, 128), f32),
            pltpu.VMEM((128, 128), f32),
        ],
        compiler_params=params,
        name="interface",
    )(near(arrived), near(book), near(slabs), near(low), near(up), near(pivot))
    answered = trade(reply)
    return pl.pallas_call(
        restore,
        out_shape=shape((LZ, LY, NX), f32),
        in_specs=[vmem] * 6,
        out_specs=hbm,
        scratch_shapes=[
            pltpu.VMEM((384, 256), f32),
            pltpu.VMEM((LZ, LY, NX), f32),
            pltpu.SemaphoreType.DMA((4,)),
        ],
        compiler_params=params,
        name="restore",
    )(near(heights), near(answered), near(kept), near(shared), near(block), near(later))


def solution(mesh):
    placed = (P("gz", "gy", None), P("gz", "gy", None), P("gz", "gy", None), P())
    return jax.shard_map(
        on_device, mesh=mesh, in_specs=placed, out_specs=P("gz", "gy", None), check_vma=False
    )
```

```python
import functools
import math

import jax
import jax.numpy as jnp
import ml_dtypes
import numpy as np
from jax import lax
from jax.experimental import pallas as pl
from jax.experimental.pallas import tpu as pltpu
from jax.sharding import PartitionSpec as P

screening = 0.0015
NX = 1024
NY = 1024
NZ = 64
GZ = 8
GY = 32
LZ = NZ // GZ
LY = NY // GY
DEV = GZ * GY
KX = NX // DEV
SMALL = 144
SHARED = 512 + 3 * SMALL
FORWARD = SHARED + 8 * 256
BACKWARD = FORWARD + 8 * 256
SLABS = BACKWARD + 512
LEAF = GY + DEV
EARLY = 6
HALF = EARLY * LY
ROWS = (HALF, (LZ + 1) * LY - HALF + 16)
BOOK = LEAF + 4 * GY * LY
f32 = jnp.float32
bf16 = jnp.bfloat16


def basis(count):
    j = np.arange(count)[:, None]
    m = np.arange(count)[None, :]
    half = count // 2
    wave = np.where(m <= half, m, m - half)
    angle = 2.0 * np.pi / count * ((j * wave) % count)
    scale = np.where((m == 0) | (m == half), 1.0, math.sqrt(2.0)) / math.sqrt(count)
    return np.where(m <= half, np.cos(angle), np.sin(angle)) * scale


def eigen(count):
    m = np.arange(count)
    half = count // 2
    wave = np.where(m <= half, m, m - half)
    return 2.0 - 2.0 * np.cos(2.0 * np.pi / count * wave)


def two(x):
    hi = np.asarray(x, np.float64).astype(ml_dtypes.bfloat16)
    lo = (x - hi.astype(np.float64)).astype(ml_dtypes.bfloat16)
    return hi, lo


@functools.lru_cache(maxsize=None)
def tables():
    half = NX // 2
    tx = basis(NX)
    ex = eigen(NX)
    columns = [
        np.concatenate([np.arange(0, half + 1, 4), half + np.arange(4, half, 4)]),
        np.concatenate([np.arange(2, half, 4), half + np.arange(2, half, 4)]),
    ]
    quarter = np.arange(256)
    turn = 2.0 * np.pi / NX * (quarter[:, None] * (4 * quarter[None, :] + 1) % NX)
    waves = math.sqrt(2.0 / NX) * np.cos(turn), math.sqrt(2.0 / NX) * np.sin(turn)
    parts = [tx[:256, columns[0]], tx[:256, columns[1]], *waves]
    lam_odd = 2.0 - 2.0 * np.cos(2.0 * np.pi / NX * (4 * quarter + 1))
    lam_x = np.stack([ex[columns[0]], ex[columns[1]], lam_odd, lam_odd])

    sine = np.zeros((LY, LY))
    sine[0, 0] = 1.0
    m = np.arange(1, LY)
    sine[1:, 1:] = math.sqrt(2.0 / LY) * np.sin(np.pi * m[:, None] * m[None, :] / LY)
    mu = np.full((LY,), 2.0)
    mu[1:] = 2.0 - 2.0 * np.cos(np.pi * m / LY)
    kron = np.kron(np.eye(LZ), sine)
    q_first = sine[:, 1].copy()
    q_first[0] = 0.0
    q_last = sine[:, LY - 1].copy()
    q_last[0] = 0.0
    mask = np.ones((LY,))
    mask[0] = 0.0
    side = np.stack([np.repeat(v[:, None], 256, axis=1) for v in (q_first, q_last, mask)])
    small = np.zeros((SMALL, 256))
    small[:KX] = lam_x
    small[16 : 16 + 3 * LY] = side.reshape(3 * LY, 256)
    small[16 + 3 * LY :] = mu[:, None] + screening
    rest, thirds = small.astype(np.float32).astype(np.float64), []
    for _ in range(3):
        thirds.append(rest.astype(ml_dtypes.bfloat16))
        rest = rest - thirds[-1].astype(np.float64)
    pack = [*two(kron), *thirds]
    for part in parts:
        pack += two(part)
    for part in parts:
        pack += two(part.T)

    ty = basis(NY)
    ey = eigen(NY)
    main = basis(GY)
    partner = np.zeros((GY, GY))
    for p in range(1, GY // 2):
        partner[:, p] = main[:, GY // 2 + p]
        partner[:, GY // 2 + p] = main[:, p]
    wave = np.where(np.arange(NY) <= NY // 2, np.arange(NY), np.arange(NY) - NY // 2)
    is_cos = np.arange(NY) <= NY // 2
    fold = wave % GY
    fold = np.minimum(fold, GY - fold)
    order = np.zeros((GY, GY), np.int64)
    for p in range(GY):
        if p in (0, GY // 2):
            order[:, p] = np.nonzero(fold == p)[0]
        elif p < GY // 2:
            order[:, p] = np.nonzero((fold == p) & is_cos)[0]
        else:
            order[:, p] = np.nonzero((fold == p - GY // 2) & ~is_cos)[0]
    shaped = ty.reshape(GY, LY, NY)[:, :, order]
    a_y = np.einsum("bvjp,bp->vjp", shaped, main)
    b_y = np.einsum("bvjp,bp->vjp", shaped, partner)
    a_m = np.einsum("mv,vjp->mjp", sine, a_y)
    b_m = np.einsum("mv,vjp->mjp", sine, b_y)
    a_m = np.tile(a_m, (1, 1, KX))
    b_m = np.tile(b_m, (1, 1, KX))
    lam_y = np.tile(ey[order], (1, KX)) + screening
    lam_d = np.repeat(lam_x.T, GY, axis=1)
    spread = np.eye(KX)
    dft = np.concatenate([np.kron(spread, main), np.kron(spread, partner)], axis=1)
    pack += two(dft)
    pack.append(np.concatenate(two(dft.T), axis=1))
    pack = np.concatenate(pack, axis=0)
    assert pack.shape == (SLABS, 256)
    later = pack[FORWARD:BACKWARD]
    both = np.stack([a_m, b_m])
    book = [lam_y, lam_d, both, both.transpose(0, 2, 1, 3)]
    book = np.concatenate([part.reshape(-1, 128) for part in book], axis=0).astype(np.float32)
    assert book.shape == (BOOK, 128)
    return pack, book, later


def split(x):
    hi = x.astype(bf16)
    return hi, (x - hi.astype(f32)).astype(bf16)


def dot(a, b):
    return lax.dot_general(a, b, (((1,), (0,)), ((), ())), preferred_element_type=f32)


def dot3(a, b):
    return dot(a[0], b[0]) + (dot(a[0], b[1]) + dot(a[1], b[0]))


def stacked3(a, count, high, low):
    full = dot(a, high)
    return full[:count] + (full[count:] + dot(a[:count], low))


def sandwich(kron, lines):
    hi, lo = split(lines)
    full = dot(kron, hi)
    count = lines.shape[0]
    return full[:count] + (full[count:] + dot(kron[:count], lo))


def wall_rows(rows, width):
    first = lax.axis_index("gz") * LZ
    inside = first + LZ < NZ
    places = [first + t for t in range(LZ)] + [jnp.minimum(first + LZ, NZ - 1)]
    heights = [jnp.concatenate([rows[pl.ds(place, 1), :]] * (width // 128), axis=1) for place in places]
    gaps = [0.5 * (heights[t] + heights[t + 1]) for t in range(LZ)]
    keep = jnp.where(inside, 1.0, 0.0).astype(f32)
    lower = [None] + [1.0 / (gaps[t - 1] * heights[t]) for t in range(1, LZ + 1)]
    upper = [1.0 / (gaps[t] * heights[t]) for t in range(LZ)]
    inverse = [1.0 / heights[t] for t in range(LZ + 1)]
    lower[LZ] = lower[LZ] * keep
    upper[LZ - 1] = upper[LZ - 1] * keep
    inverse[LZ] = inverse[LZ] * keep
    return lower, upper, inverse


def block_pivots(off, mask, lower, upper):
    pivots = [None] * LZ
    for t in range(1, LZ):
        diagonal = off + (lower[t] + upper[t])
        if t > 1:
            diagonal = diagonal - (lower[t] * upper[t - 1]) * pivots[t - 1]
        pivots[t] = mask / diagonal
    return pivots


def block_solve(right, pivots, lower, upper):
    value = [None] * LZ
    for t in range(1, LZ):
        term = right[t] if t == 1 else right[t] + lower[t] * value[t - 1]
        value[t] = term * pivots[t]
    for t in range(LZ - 2, 0, -1):
        value[t] = value[t] + upper[t] * pivots[t] * value[t + 1]
    return value


def eliminate(
    spacing_in, stream_in, span_in, wall_in, pack_in, book_in,
    message, kept, heights, book, slabs, low, up, pivot, block, shared, lead, gain,
    spacing, stream, span, wall, pack, part_0, part_1, part_2, part_3, part_4, part_5, ends, cell_sem, table_sem,
):
    first_copy = pltpu.make_async_copy(spacing_in, spacing, table_sem.at[0])
    first_copy.start()
    leaf = pltpu.make_async_copy(book_in.at[pl.ds(0, LEAF)], book.at[pl.ds(0, LEAF)], table_sem.at[4])
    leaf.start()
    copies = []
    for t in range(0, LZ, 2):
        here = pl.ds(t, 2)
        trio = [
            pltpu.make_async_copy(source.at[here], target.at[here], cell_sem.at[t // 2, k])
            for k, (source, target) in enumerate(((stream_in, stream), (span_in, span), (wall_in, wall)))
        ]
        for copy in trio:
            copy.start()
        copies.append(trio)
        if t == 2:
            table_copies = []
            moves = (
                (pack_in.at[pl.ds(0, SHARED)], shared),
                (pack_in.at[pl.ds(SHARED, 1024)], pack.at[pl.ds(0, 1024)]),
                (pack_in.at[pl.ds(SHARED + 1024, 1024)], pack.at[pl.ds(1024, 1024)]),
            )
            for k, (source, target) in enumerate(moves):
                table_copies.append(pltpu.make_async_copy(source, target, table_sem.at[k + 1]))
                table_copies[-1].start()
    ahead = [
        pltpu.make_async_copy(pack_in.at[pl.ds(BACKWARD, 512)], slabs, table_sem.at[5]),
        pltpu.make_async_copy(
            book_in.at[pl.ds(LEAF, BOOK - LEAF)], book.at[pl.ds(LEAF, BOOK - LEAF)], table_sem.at[6]
        ),
    ]
    for copy in ahead:
        copy.start()
    first_copy.wait()
    for z in range(NZ):
        heights[z : z + 1, :] = jnp.full((1, 128), spacing[z], f32)
    tall = heights[...]
    layer = lax.broadcasted_iota(jnp.int32, (NZ, 128), 0)
    gap = 0.5 * (tall + pltpu.roll(tall, NZ - 1, axis=0))
    low[...] = jnp.where(layer == 0, 0.0, 1.0 / (pltpu.roll(gap, 1, axis=0) * tall))
    up[...] = jnp.where(layer == NZ - 1, 0.0, 1.0 / (gap * tall))
    leaf.wait()
    me = lax.axis_index("gy") * GZ + lax.axis_index("gz")
    off = book[pl.ds(0, GY), :] + book[pl.ds(GY + me, 1), :]
    half = NZ // 2
    last = [None, None]

    def wall_step(s):
        for side, z in enumerate((s, NZ - 1 - s)):
            diagonal = off + (low[z : z + 1, :] + up[z : z + 1, :])
            if s > 0 and side == 0:
                diagonal = diagonal - (low[z : z + 1, :] * up[z - 1 : z, :]) * last[0]
            if s > 0 and side == 1:
                diagonal = diagonal - (up[z : z + 1, :] * low[z + 1 : z + 2, :]) * last[1]
            last[side] = 1.0 / diagonal
            pivot[z] = last[side]
            lead[z] = (low, up)[side][z : z + 1, :] * last[side]
            gain[z] = (up, low)[side][z : z + 1, :] * last[side]

    lower, upper, inverse = wall_rows(heights, NX)
    rows = lax.broadcasted_iota(jnp.int32, (LY, NX), 0)
    extra = []

    def transform(part, wave):
        first = 512 * wave
        return stacked3(part[...], part.shape[0] // 2, pack[first : first + 256, :], pack[first + 256 : first + 512, :])

    def transform_group(parts, group):
        count = ROWS[group]
        lines = [transform(parts[0], 0), transform(parts[1], 1)]
        cosine, sine = transform(parts[2], 2), transform(parts[2], 3)
        lines += [cosine[:count] - sine[count:], sine[:count] + cosine[count:]]
        size = (HALF, LZ * LY - HALF)[group]
        sines = shared[:size, :size], shared[256 : 256 + size, :size]
        for i in range(KX):
            kept[i, group * HALF : group * HALF + size, :] = dot3(sines, split(lines[i][:size]))
            if group == 1:
                crown = dot3((sines[0][:LY, :LY], sines[1][:LY, :LY]), split(lines[i][size : size + LY]))
                extra.append((crown, lines[i][size + LY : size + LY + LZ]))

    for t in range(LZ + 2):
        if t < LZ:
            if t % 2 == 0:
                for copy in copies[t // 2]:
                    copy.wait()
            u = stream[t]
            v = span[t]
            w = wall[t]
            shifted = jnp.where(rows == 0, 0.0, pltpu.roll(v, 1, axis=0))
            d = (pltpu.roll(u, 1, axis=1) - u) + (shifted - v)
            d = d - w * inverse[t] if t == 0 else d + (wall[t - 1] - w) * inverse[t]
        elif t == LZ:
            d = wall[LZ - 1] * inverse[LZ]
        else:
            d = jnp.concatenate([span[z, LY - 1 :, :] for z in range(LZ)] + [jnp.zeros((8, NX), f32)], axis=0)
        even = d[:, :512] + d[:, 512:]
        odd = d[:, :512] - d[:, 512:]
        pieces = (even[:, :256] + even[:, 256:], even[:, :256] - even[:, 256:], odd[:, :256], odd[:, 256:])
        for k, piece in enumerate(pieces):
            hi, lo = split(piece)
            group = 0 if t < EARLY else 1
            count = ROWS[group]
            parts = ((part_0, part_1, part_2, part_2), (part_3, part_4, part_5, part_5))[group]
            for part, level in ((hi, 0), (lo, 1)):
                first = (level, level, 2 * level, 2 * level + 1)[k] * count + t * LY - group * HALF
                parts[k][first : first + d.shape[0], :] = part
        if t < LZ:
            for step in range(half * t // LZ, half * (t + 1) // LZ):
                wall_step(step)
        if t == EARLY - 1:
            for copy in table_copies:
                copy.wait()
            transform_group((part_0, part_1, part_2), 0)
    transform_group((part_3, part_4, part_5), 1)
    lower, upper, inverse = wall_rows(heights, 256)
    small = sum(shared[512 + k * SMALL : 512 + (k + 1) * SMALL, :].astype(f32) for k in range(3))
    q_first, q_last, mask, mu = (small[16 + k * LY : 16 + (k + 1) * LY] for k in range(4))
    for i in range(KX):
        cells = kept[i]
        crown, edge = extra[i]
        layers = [cells[t * LY : (t + 1) * LY] for t in range(LZ)]
        pivots = block_pivots(mu + small[i : i + 1], mask, lower, upper)
        for t in range(1, LZ):
            block[i, (t - 1) * LY : t * LY, :] = pivots[t]
        inner = block_solve(layers, pivots, lower, upper)
        ends[i * LY : (i + 1) * LY, :] = layers[0] + upper[0] * inner[1]
        ends[128 + i * LY : 128 + (i + 1) * LY, :] = crown + lower[LZ] * inner[LZ - 1]
        own = [jnp.zeros((1, 256), f32)]
        following = [jnp.zeros((1, 256), f32)]
        for t in range(1, LZ):
            own.append(layers[t][:1] + jnp.sum(inner[t] * q_first, axis=0, keepdims=True))
            following.append(jnp.sum(inner[t] * q_last, axis=0, keepdims=True))
        ends[256 + i * LZ : 256 + (i + 1) * LZ, :] = jnp.concatenate(own, axis=0)
        ends[320 + i * LZ : 320 + (i + 1) * LZ, :] = edge + jnp.concatenate(following, axis=0)
    ends[256 + KX * LZ : 320, :] = jnp.zeros((64 - KX * LZ, 256), f32)
    ends[320 + KX * LZ : 384, :] = jnp.zeros((64 - KX * LZ, 256), f32)
    for r in range(3):
        message[pl.ds(r, DEV, stride=3), :] = ends[128 * r : 128 * (r + 1), :].T
    for copy in ahead:
        copy.wait()


def interface(
    arrived, book, slabs, lead, gain, pivot, reply, value, spec, lines, top, back,
):
    dft_hi, dft_lo, idft = slabs[:128, :], slabs[128:256, :], slabs[256:, :]
    idft_hi, idft_lo = idft[:, :128], idft[:, 128:]
    fwd = lambda k, m: book[pl.ds(LEAF + (k * LY + m) * GY, GY), :]
    inv = lambda k, j: book[pl.ds(LEAF + 2 * LY * GY + (k * GY + j) * LY, LY), :]
    half = NZ // 2
    lane = lax.broadcasted_iota(jnp.int32, (GY, 128), 1)
    field = [arrived[pl.ds(3 * a, GY, stride=3 * GZ), :] for a in range(GZ)]
    for a in range(1, GZ):
        field[a] = field[a] + arrived[pl.ds(3 * (a - 1) + 1, GY, stride=3 * GZ), :]
    for g in range(2):
        blocks = []
        for i in range(KX):
            block = None
            for k in range(4):
                moved = pltpu.roll(field[4 * g + k], (32 * (k - i)) % 128, axis=1)
                block = moved if block is None else jnp.where(lane // 32 == k, moved, block)
            blocks.append(block)
        stacked = jnp.concatenate(blocks, axis=0).T
        spec[128 * g : 128 * (g + 1), :] = dot3(split(stacked), (dft_hi, dft_lo))
    sides = []
    for a in range(GZ):
        rest = arrived[pl.ds(3 * a + 2, GY, stride=3 * GZ), :]
        sides.append(rest + pltpu.roll(pltpu.roll(rest, 64, axis=1), 1, axis=0))
    blocks = []
    for i in range(KX):
        block = jnp.zeros((GY, 128), f32)
        for a in range(GZ):
            moved = pltpu.roll(sides[a], (8 * (a - i)) % 128, axis=1)
            block = jnp.where(lane // 8 == a, moved, block)
        blocks.append(block)
    stacked = jnp.concatenate(blocks, axis=0).T[:NZ]
    lines[...] = dot3(split(stacked), (dft_hi[:, :128], dft_lo[:, :128]))
    for g in range(2):
        total = [jnp.zeros((GY, 128), f32)] * 4
        for m in range(LY):
            c_main = fwd(0, m)
            c_partner = fwd(1, m)
            for k in range(4):
                row = 128 * g + 32 * k + m
                total[k] = total[k] + c_main * spec[row : row + 1, :128] + c_partner * spec[row : row + 1, 128:]
        for k in range(4):
            top[4 * g + k] = total[k]
    weight = fwd(0, 0)
    for s in range(half):
        for z in (s, NZ - 1 - s):
            right = weight * lines[z : z + 1, :]
            if z % LZ == 0:
                right = right + top[z // LZ]
            now = right * pivot[z]
            if s > 0:
                now = now + lead[z] * value[z - 1 if z < half else z + 1]
            value[z] = now
    alpha = gain[half - 1]
    beta = gain[half]
    below = (value[half - 1] + alpha * value[half]) / (1.0 - alpha * beta)
    above = value[half] + beta * below
    for s in range(half):
        for z in (half - 1 - s, half + s):
            if z < half:
                if s > 0:
                    below = value[z] + gain[z] * below
                now = below
            else:
                if s > 0:
                    above = value[z] + gain[z] * above
                now = above
            lines[z : z + 1, :] = jnp.sum(now * weight, axis=0, keepdims=True)
            if z % LZ == 0:
                top[z // LZ] = now
    for g in range(2):
        total = [jnp.zeros((LY, 128), f32)] * 4
        other = [jnp.zeros((LY, 128), f32)] * 4
        for j in range(GY):
            c_main = inv(0, j)
            c_partner = inv(1, j)
            for k in range(4):
                row = top[4 * g + k, j : j + 1, :]
                total[k] = total[k] + c_main * row
                other[k] = other[k] + c_partner * row
        for k in range(4):
            spec[128 * g + 32 * k : 128 * g + 32 * (k + 1), :128] = total[k]
            spec[128 * g + 32 * k : 128 * g + 32 * (k + 1), 128:] = other[k]
    for g in range(2):
        back[...] = dot3(split(spec[128 * g : 128 * (g + 1), :]), (idft_hi, idft_lo)).T
        for k in range(4):
            block = None
            for i in range(KX):
                moved = pltpu.roll(back[32 * i : 32 * (i + 1), :], (32 * (i - k)) % 128, axis=1)
                block = moved if block is None else jnp.where(lane // 32 == i, moved, block)
            a = 4 * g + k
            reply[pl.ds(3 * a, GY, stride=3 * GZ), :] = block
            if a > 0:
                reply[pl.ds(3 * (a - 1) + 1, GY, stride=3 * GZ), :] = block
    reply[pl.ds(3 * (GZ - 1) + 1, GY, stride=3 * GZ), :] = jnp.zeros((GY, 128), f32)
    rest = dot3(split(lines[...]), (idft_hi[:128, :], idft_lo[:128, :]))
    back[...] = jnp.concatenate([rest, rest], axis=0).T
    pieces = []
    for i in range(KX):
        piece = back[32 * i : 32 * (i + 1), :]
        pieces.append(jnp.where(lane < 64, piece, pltpu.roll(piece, GY - 1, axis=0)))
    for a in range(GZ):
        block = jnp.zeros((GY, 128), f32)
        for i in range(KX):
            moved = pltpu.roll(pieces[i], (8 * (i - a)) % 128, axis=1)
            block = jnp.where((lane % 64) // 8 == i, moved, block)
        reply[pl.ds(3 * a + 2, GY, stride=3 * GZ), :] = block


def restore(
    rows, arrived, kept, shared, block, pack, pressure, ends, result, out_sem,
):
    lower, upper, _ = wall_rows(rows, 256)
    small = sum(shared[512 + k * SMALL : 512 + (k + 1) * SMALL, :].astype(f32) for k in range(3))
    q_first, q_last, mask = (small[16 + k * LY : 16 + (k + 1) * LY] for k in range(3))
    for r in range(3):
        ends[128 * r : 128 * (r + 1), :] = arrived[pl.ds(r, DEV, stride=3), :].T
    lines = []
    for i in range(KX):
        floor = ends[i * LY : (i + 1) * LY, :]
        ceiling = ends[128 + i * LY : 128 + (i + 1) * LY, :]
        pivots = [None] + [block[i, (t - 1) * LY : t * LY, :] for t in range(1, LZ)]
        right = [None] * LZ
        near = [None] * LZ
        for t in range(1, LZ):
            near[t] = ends[256 + i * LZ + t : 256 + i * LZ + t + 1, :]
            far = ends[320 + i * LZ + t : 320 + i * LZ + t + 1, :]
            right[t] = kept[i, t * LY : (t + 1) * LY, :] + (q_first * near[t] + q_last * far)
        right[1] = right[1] + lower[1] * floor
        right[LZ - 1] = right[LZ - 1] + upper[LZ - 1] * ceiling
        inner = block_solve(right, pivots, lower, upper)
        layers = [floor] + [inner[t] + (1.0 - mask) * near[t] for t in range(1, LZ)]
        modes = jnp.concatenate(layers, axis=0)
        lines.append(sandwich(shared[:512, :], modes))

    def transform(line, wave):
        first = 512 * wave
        return dot3(line, (pack[first : first + 256, :], pack[first + 256 : first + 512, :]))

    minus = split(-lines[2])
    lines = [split(line) for line in lines]
    even = transform(lines[0], 0)
    odd = transform(lines[1], 1)
    copies = []
    for q in range(2):
        if q == 0:
            whole = even + odd
            swing = transform(lines[2], 2) + transform(lines[3], 3)
        else:
            whole = even - odd
            swing = transform(minus, 3) + transform(lines[3], 2)
        for k, piece in ((q, whole + swing), (q + 2, whole - swing)):
            here = pl.ds(256 * k, 256)
            result[:, :, 256 * k : 256 * (k + 1)] = piece.reshape(LZ, LY, 256)
            copy = pltpu.make_async_copy(result.at[:, :, here], pressure.at[:, :, here], out_sem.at[k])
            copy.start()
            copies.append(copy)
    for copy in copies:
        copy.wait()


def on_device(streamwise, spanwise, wall_normal, spacing):
    far = lambda x: pltpu.with_memory_space_constraint(x, pltpu.HBM)
    near = lambda x: pltpu.with_memory_space_constraint(x, pltpu.VMEM)
    pack, book, later = (jnp.asarray(part) for part in tables())
    pack, book = far(pack), far(book)
    vmem = pl.BlockSpec(memory_space=pltpu.VMEM)
    hbm = pl.BlockSpec(memory_space=pltpu.HBM)
    params = pltpu.CompilerParams(vmem_limit_bytes=50 * 2**20)
    shape = jax.ShapeDtypeStruct
    message, kept, heights, book, slabs, low, up, pivot, block, shared, lead, gain = pl.pallas_call(
        eliminate,
        out_shape=(
            pltpu.VMEM((3 * DEV, 128), f32),
            pltpu.VMEM((KX, LZ * LY, 256), f32),
            pltpu.VMEM((NZ, 128), f32),
            pltpu.VMEM((BOOK, 128), f32),
            pltpu.VMEM((512, 256), bf16),
            pltpu.VMEM((NZ, 128), f32),
            pltpu.VMEM((NZ, 128), f32),
            pltpu.VMEM((NZ, GY, 128), f32),
            pltpu.VMEM((KX, (LZ - 1) * LY, 256), f32),
            pltpu.VMEM((SHARED, 256), bf16),
            pltpu.VMEM((NZ, GY, 128), f32),
            pltpu.VMEM((NZ, GY, 128), f32),
        ),
        in_specs=[hbm] * 6,
        out_specs=(vmem,) * 12,
        scratch_shapes=[
            pltpu.SMEM((NZ,), f32),
            pltpu.VMEM((LZ, LY, NX), f32),
            pltpu.VMEM((LZ, LY, NX), f32),
            pltpu.VMEM((LZ, LY, NX), f32),
            pltpu.VMEM((8 * 256, 256), bf16),
            pltpu.VMEM((2 * ROWS[0], 256), bf16),
            pltpu.VMEM((2 * ROWS[0], 256), bf16),
            pltpu.VMEM((4 * ROWS[0], 256), bf16),
            pltpu.VMEM((2 * ROWS[1], 256), bf16),
            pltpu.VMEM((2 * ROWS[1], 256), bf16),
            pltpu.VMEM((4 * ROWS[1], 256), bf16),
            pltpu.VMEM((384, 256), f32),
            pltpu.SemaphoreType.DMA((LZ // 2, 3)),
            pltpu.SemaphoreType.DMA((7,)),
        ],
        compiler_params=params,
        name="eliminate",
    )(far(spacing), far(streamwise), far(spanwise), far(wall_normal), pack, book)
    axes = ("gy", "gz")
    trade = lambda x: lax.all_to_all(
        x.reshape(DEV, 1, 384), axes, split_axis=0, concat_axis=0, tiled=True
    ).reshape(3 * DEV, 128)
    arrived = trade(message)
    reply = pl.pallas_call(
        interface,
        out_shape=pltpu.VMEM((3 * DEV, 128), f32),
        in_specs=[vmem] * 6,
        out_specs=vmem,
        scratch_shapes=[
            pltpu.VMEM((NZ, GY, 128), f32),
            pltpu.VMEM((256, 256), f32),
            pltpu.VMEM((NZ, 128), f32),
            pltpu.VMEM((GZ, GY, 128), f32),
            pltpu.VMEM((128, 128), f32),
        ],
        compiler_params=params,
        name="interface",
    )(near(arrived), near(book), near(slabs), near(lead), near(gain), near(pivot))
    answered = trade(reply)
    return pl.pallas_call(
        restore,
        out_shape=shape((LZ, LY, NX), f32),
        in_specs=[vmem] * 6,
        out_specs=hbm,
        scratch_shapes=[
            pltpu.VMEM((384, 256), f32),
            pltpu.VMEM((LZ, LY, NX), f32),
            pltpu.SemaphoreType.DMA((4,)),
        ],
        compiler_params=params,
        name="restore",
    )(near(heights), near(answered), near(kept), near(shared), near(block), near(later))


def solution(mesh):
    placed = (P("gz", "gy", None), P("gz", "gy", None), P("gz", "gy", None), P())
    return jax.shard_map(
        on_device, mesh=mesh, in_specs=placed, out_specs=P("gz", "gy", None), check_vma=False
    )
```

```python
import functools
import math

import jax
import jax.numpy as jnp
import ml_dtypes
import numpy as np
from jax import lax
from jax.experimental import pallas as pl
from jax.experimental.pallas import tpu as pltpu
from jax.sharding import PartitionSpec as P

screening = 0.0015
NX = 1024
NY = 1024
NZ = 64
GZ = 8
GY = 32
LZ = NZ // GZ
LY = NY // GY
DEV = GZ * GY
KX = NX // DEV
SMALL = 144
SHARED = 512 + 3 * SMALL
FORWARD = SHARED + 8 * 256
BACKWARD = FORWARD + 8 * 256
SLABS = BACKWARD + 512
LEAF = GY + DEV
EARLY = 6
HALF = EARLY * LY
ROWS = (HALF, (LZ + 1) * LY - HALF + 16)
BOOK = LEAF + 4 * GY * LY
f32 = jnp.float32
bf16 = jnp.bfloat16


def basis(count):
    j = np.arange(count)[:, None]
    m = np.arange(count)[None, :]
    half = count // 2
    wave = np.where(m <= half, m, m - half)
    angle = 2.0 * np.pi / count * ((j * wave) % count)
    scale = np.where((m == 0) | (m == half), 1.0, math.sqrt(2.0)) / math.sqrt(count)
    return np.where(m <= half, np.cos(angle), np.sin(angle)) * scale


def eigen(count):
    m = np.arange(count)
    half = count // 2
    wave = np.where(m <= half, m, m - half)
    return 2.0 - 2.0 * np.cos(2.0 * np.pi / count * wave)


def two(x):
    hi = np.asarray(x, np.float64).astype(ml_dtypes.bfloat16)
    lo = (x - hi.astype(np.float64)).astype(ml_dtypes.bfloat16)
    return hi, lo


@functools.lru_cache(maxsize=None)
def tables():
    half = NX // 2
    tx = basis(NX)
    ex = eigen(NX)
    columns = [
        np.concatenate([np.arange(0, half + 1, 4), half + np.arange(4, half, 4)]),
        np.concatenate([np.arange(2, half, 4), half + np.arange(2, half, 4)]),
    ]
    quarter = np.arange(256)
    turn = 2.0 * np.pi / NX * (quarter[:, None] * (4 * quarter[None, :] + 1) % NX)
    waves = math.sqrt(2.0 / NX) * np.cos(turn), math.sqrt(2.0 / NX) * np.sin(turn)
    parts = [tx[:256, columns[0]], tx[:256, columns[1]], *waves]
    lam_odd = 2.0 - 2.0 * np.cos(2.0 * np.pi / NX * (4 * quarter + 1))
    lam_x = np.stack([ex[columns[0]], ex[columns[1]], lam_odd, lam_odd])

    sine = np.zeros((LY, LY))
    sine[0, 0] = 1.0
    m = np.arange(1, LY)
    sine[1:, 1:] = math.sqrt(2.0 / LY) * np.sin(np.pi * m[:, None] * m[None, :] / LY)
    mu = np.full((LY,), 2.0)
    mu[1:] = 2.0 - 2.0 * np.cos(np.pi * m / LY)
    kron = np.kron(np.eye(LZ), sine)
    q_first = sine[:, 1].copy()
    q_first[0] = 0.0
    q_last = sine[:, LY - 1].copy()
    q_last[0] = 0.0
    mask = np.ones((LY,))
    mask[0] = 0.0
    side = np.stack([np.repeat(v[:, None], 256, axis=1) for v in (q_first, q_last, mask)])
    small = np.zeros((SMALL, 256))
    small[:KX] = lam_x
    small[16 : 16 + 3 * LY] = side.reshape(3 * LY, 256)
    small[16 + 3 * LY :] = mu[:, None] + screening
    rest, thirds = small.astype(np.float32).astype(np.float64), []
    for _ in range(3):
        thirds.append(rest.astype(ml_dtypes.bfloat16))
        rest = rest - thirds[-1].astype(np.float64)
    pack = [*two(kron), *thirds]
    for part in parts:
        pack += two(part)
    for part in parts:
        pack += two(part.T)

    ty = basis(NY)
    ey = eigen(NY)
    main = basis(GY)
    partner = np.zeros((GY, GY))
    for p in range(1, GY // 2):
        partner[:, p] = main[:, GY // 2 + p]
        partner[:, GY // 2 + p] = main[:, p]
    wave = np.where(np.arange(NY) <= NY // 2, np.arange(NY), np.arange(NY) - NY // 2)
    is_cos = np.arange(NY) <= NY // 2
    fold = wave % GY
    fold = np.minimum(fold, GY - fold)
    order = np.zeros((GY, GY), np.int64)
    for p in range(GY):
        if p in (0, GY // 2):
            order[:, p] = np.nonzero(fold == p)[0]
        elif p < GY // 2:
            order[:, p] = np.nonzero((fold == p) & is_cos)[0]
        else:
            order[:, p] = np.nonzero((fold == p - GY // 2) & ~is_cos)[0]
    shaped = ty.reshape(GY, LY, NY)[:, :, order]
    a_y = np.einsum("bvjp,bp->vjp", shaped, main)
    b_y = np.einsum("bvjp,bp->vjp", shaped, partner)
    a_m = np.einsum("mv,vjp->mjp", sine, a_y)
    b_m = np.einsum("mv,vjp->mjp", sine, b_y)
    a_m = np.tile(a_m, (1, 1, KX))
    b_m = np.tile(b_m, (1, 1, KX))
    lam_y = np.tile(ey[order], (1, KX)) + screening
    lam_d = np.repeat(lam_x.T, GY, axis=1)
    spread = np.eye(KX)
    dft = np.concatenate([np.kron(spread, main), np.kron(spread, partner)], axis=1)
    pack += two(dft)
    pack.append(np.concatenate(two(dft.T), axis=1))
    pack = np.concatenate(pack, axis=0)
    assert pack.shape == (SLABS, 256)
    later = pack[FORWARD:BACKWARD]
    both = np.stack([a_m, b_m])
    book = [lam_y, lam_d, both, both.transpose(0, 2, 1, 3)]
    book = np.concatenate([part.reshape(-1, 128) for part in book], axis=0).astype(np.float32)
    assert book.shape == (BOOK, 128)
    return pack, book, later


def split(x):
    hi = x.astype(bf16)
    return hi, (x - hi.astype(f32)).astype(bf16)


def dot(a, b):
    return lax.dot_general(a, b, (((1,), (0,)), ((), ())), preferred_element_type=f32)


def dot3(a, b):
    return dot(a[0], b[0]) + (dot(a[0], b[1]) + dot(a[1], b[0]))


def stacked3(a, count, high, low):
    full = dot(a, high)
    return full[:count] + (full[count:] + dot(a[:count], low))


def sandwich(kron, lines):
    hi, lo = split(lines)
    full = dot(kron, hi)
    count = lines.shape[0]
    return full[:count] + (full[count:] + dot(kron[:count], lo))


def wall_rows(rows, width):
    first = lax.axis_index("gz") * LZ
    inside = first + LZ < NZ
    places = [first + t for t in range(LZ)] + [jnp.minimum(first + LZ, NZ - 1)]
    heights = [jnp.concatenate([rows[pl.ds(place, 1), :]] * (width // 128), axis=1) for place in places]
    gaps = [0.5 * (heights[t] + heights[t + 1]) for t in range(LZ)]
    keep = jnp.where(inside, 1.0, 0.0).astype(f32)
    lower = [None] + [1.0 / (gaps[t - 1] * heights[t]) for t in range(1, LZ + 1)]
    upper = [1.0 / (gaps[t] * heights[t]) for t in range(LZ)]
    inverse = [1.0 / heights[t] for t in range(LZ + 1)]
    lower[LZ] = lower[LZ] * keep
    upper[LZ - 1] = upper[LZ - 1] * keep
    inverse[LZ] = inverse[LZ] * keep
    return lower, upper, inverse


def block_pivots(off, mask, lower, upper):
    pivots = [None] * LZ
    for t in range(1, LZ):
        diagonal = off + (lower[t] + upper[t])
        if t > 1:
            diagonal = diagonal - (lower[t] * upper[t - 1]) * pivots[t - 1]
        pivots[t] = mask / diagonal
    return pivots


def block_solve(right, pivots, lower, upper):
    value = [None] * LZ
    for t in range(1, LZ):
        term = right[t] if t == 1 else right[t] + lower[t] * value[t - 1]
        value[t] = term * pivots[t]
    for t in range(LZ - 2, 0, -1):
        value[t] = value[t] + upper[t] * pivots[t] * value[t + 1]
    return value


def eliminate(
    spacing_in, stream_in, span_in, wall_in, pack_in, book_in,
    message, kept, heights, book, slabs, low, up, pivot, block, shared,
    spacing, stream, span, wall, pack, part_0, part_1, part_2, part_3, part_4, part_5, ends, cell_sem, table_sem,
):
    first_copy = pltpu.make_async_copy(spacing_in, spacing, table_sem.at[0])
    first_copy.start()
    leaf = pltpu.make_async_copy(book_in.at[pl.ds(0, LEAF)], book.at[pl.ds(0, LEAF)], table_sem.at[4])
    leaf.start()
    copies = []
    for t in range(0, LZ, 2):
        here = pl.ds(t, 2)
        trio = [
            pltpu.make_async_copy(source.at[here], target.at[here], cell_sem.at[t // 2, k])
            for k, (source, target) in enumerate(((stream_in, stream), (span_in, span), (wall_in, wall)))
        ]
        for copy in trio:
            copy.start()
        copies.append(trio)
        if t == 2:
            table_copies = []
            moves = (
                (pack_in.at[pl.ds(0, SHARED)], shared),
                (pack_in.at[pl.ds(SHARED, 1024)], pack.at[pl.ds(0, 1024)]),
                (pack_in.at[pl.ds(SHARED + 1024, 1024)], pack.at[pl.ds(1024, 1024)]),
            )
            for k, (source, target) in enumerate(moves):
                table_copies.append(pltpu.make_async_copy(source, target, table_sem.at[k + 1]))
                table_copies[-1].start()
    ahead = [
        pltpu.make_async_copy(pack_in.at[pl.ds(BACKWARD, 512)], slabs, table_sem.at[5]),
        pltpu.make_async_copy(
            book_in.at[pl.ds(LEAF, BOOK - LEAF)], book.at[pl.ds(LEAF, BOOK - LEAF)], table_sem.at[6]
        ),
    ]
    for copy in ahead:
        copy.start()
    first_copy.wait()
    for z in range(NZ):
        heights[z : z + 1, :] = jnp.full((1, 128), spacing[z], f32)
    tall = heights[...]
    layer = lax.broadcasted_iota(jnp.int32, (NZ, 128), 0)
    gap = 0.5 * (tall + pltpu.roll(tall, NZ - 1, axis=0))
    low[...] = jnp.where(layer == 0, 0.0, 1.0 / (pltpu.roll(gap, 1, axis=0) * tall))
    up[...] = jnp.where(layer == NZ - 1, 0.0, 1.0 / (gap * tall))
    leaf.wait()
    me = lax.axis_index("gy") * GZ + lax.axis_index("gz")
    off = book[pl.ds(0, GY), :] + book[pl.ds(GY + me, 1), :]
    half = NZ // 2
    last = [None, None]

    def wall_step(s):
        for side, z in enumerate((s, NZ - 1 - s)):
            diagonal = off + (low[z : z + 1, :] + up[z : z + 1, :])
            if s > 0 and side == 0:
                diagonal = diagonal - (low[z : z + 1, :] * up[z - 1 : z, :]) * last[0]
            if s > 0 and side == 1:
                diagonal = diagonal - (up[z : z + 1, :] * low[z + 1 : z + 2, :]) * last[1]
            last[side] = 1.0 / diagonal
            pivot[z] = last[side]

    lower, upper, inverse = wall_rows(heights, NX)
    rows = lax.broadcasted_iota(jnp.int32, (LY, NX), 0)
    extra = []

    def transform(part, wave):
        first = 512 * wave
        return stacked3(part[...], part.shape[0] // 2, pack[first : first + 256, :], pack[first + 256 : first + 512, :])

    def transform_group(parts, group):
        count = ROWS[group]
        lines = [transform(parts[0], 0), transform(parts[1], 1)]
        cosine, sine = transform(parts[2], 2), transform(parts[2], 3)
        lines += [cosine[:count] - sine[count:], sine[:count] + cosine[count:]]
        size = (HALF, LZ * LY - HALF)[group]
        sines = shared[:size, :size], shared[256 : 256 + size, :size]
        for i in range(KX):
            kept[i, group * HALF : group * HALF + size, :] = dot3(sines, split(lines[i][:size]))
            if group == 1:
                crown = dot3((sines[0][:LY, :LY], sines[1][:LY, :LY]), split(lines[i][size : size + LY]))
                extra.append((crown, lines[i][size + LY : size + LY + LZ]))

    for t in range(LZ + 2):
        if t < LZ:
            if t % 2 == 0:
                for copy in copies[t // 2]:
                    copy.wait()
            u = stream[t]
            v = span[t]
            w = wall[t]
            shifted = jnp.where(rows == 0, 0.0, pltpu.roll(v, 1, axis=0))
            d = (pltpu.roll(u, 1, axis=1) - u) + (shifted - v)
            d = d - w * inverse[t] if t == 0 else d + (wall[t - 1] - w) * inverse[t]
        elif t == LZ:
            d = wall[LZ - 1] * inverse[LZ]
        else:
            d = jnp.concatenate([span[z, LY - 1 :, :] for z in range(LZ)] + [jnp.zeros((8, NX), f32)], axis=0)
        even = d[:, :512] + d[:, 512:]
        odd = d[:, :512] - d[:, 512:]
        pieces = (even[:, :256] + even[:, 256:], even[:, :256] - even[:, 256:], odd[:, :256], odd[:, 256:])
        for k, piece in enumerate(pieces):
            hi, lo = split(piece)
            group = 0 if t < EARLY else 1
            count = ROWS[group]
            parts = ((part_0, part_1, part_2, part_2), (part_3, part_4, part_5, part_5))[group]
            for part, level in ((hi, 0), (lo, 1)):
                first = (level, level, 2 * level, 2 * level + 1)[k] * count + t * LY - group * HALF
                parts[k][first : first + d.shape[0], :] = part
        if t < LZ:
            for step in range(half * t // LZ, half * (t + 1) // LZ):
                wall_step(step)
        if t == EARLY - 1:
            for copy in table_copies:
                copy.wait()
            transform_group((part_0, part_1, part_2), 0)
    transform_group((part_3, part_4, part_5), 1)
    lower, upper, inverse = wall_rows(heights, 256)
    small = sum(shared[512 + k * SMALL : 512 + (k + 1) * SMALL, :].astype(f32) for k in range(3))
    q_first, q_last, mask, mu = (small[16 + k * LY : 16 + (k + 1) * LY] for k in range(4))
    for i in range(KX):
        cells = kept[i]
        crown, edge = extra[i]
        layers = [cells[t * LY : (t + 1) * LY] for t in range(LZ)]
        pivots = block_pivots(mu + small[i : i + 1], mask, lower, upper)
        for t in range(1, LZ):
            block[i, (t - 1) * LY : t * LY, :] = pivots[t]
        inner = block_solve(layers, pivots, lower, upper)
        ends[i * LY : (i + 1) * LY, :] = layers[0] + upper[0] * inner[1]
        ends[128 + i * LY : 128 + (i + 1) * LY, :] = crown + lower[LZ] * inner[LZ - 1]
        own = [jnp.zeros((1, 256), f32)]
        following = [jnp.zeros((1, 256), f32)]
        for t in range(1, LZ):
            own.append(layers[t][:1] + jnp.sum(inner[t] * q_first, axis=0, keepdims=True))
            following.append(jnp.sum(inner[t] * q_last, axis=0, keepdims=True))
        ends[256 + i * LZ : 256 + (i + 1) * LZ, :] = jnp.concatenate(own, axis=0)
        ends[320 + i * LZ : 320 + (i + 1) * LZ, :] = edge + jnp.concatenate(following, axis=0)
    ends[256 + KX * LZ : 320, :] = jnp.zeros((64 - KX * LZ, 256), f32)
    ends[320 + KX * LZ : 384, :] = jnp.zeros((64 - KX * LZ, 256), f32)
    for r in range(3):
        message[pl.ds(r, DEV, stride=3), :] = ends[128 * r : 128 * (r + 1), :].T
    for copy in ahead:
        copy.wait()


def interface(
    arrived, book, slabs, low, up, pivot, reply, value, spec, lines, top, back,
):
    dft_hi, dft_lo, idft = slabs[:128, :], slabs[128:256, :], slabs[256:, :]
    idft_hi, idft_lo = idft[:, :128], idft[:, 128:]
    fwd = lambda k, m: book[pl.ds(LEAF + (k * LY + m) * GY, GY), :]
    inv = lambda k, j: book[pl.ds(LEAF + 2 * LY * GY + (k * GY + j) * LY, LY), :]
    half = NZ // 2
    lane = lax.broadcasted_iota(jnp.int32, (GY, 128), 1)
    field = [arrived[pl.ds(3 * a, GY, stride=3 * GZ), :] for a in range(GZ)]
    for a in range(1, GZ):
        field[a] = field[a] + arrived[pl.ds(3 * (a - 1) + 1, GY, stride=3 * GZ), :]
    for g in range(2):
        blocks = []
        for i in range(KX):
            block = None
            for k in range(4):
                moved = pltpu.roll(field[4 * g + k], (32 * (k - i)) % 128, axis=1)
                block = moved if block is None else jnp.where(lane // 32 == k, moved, block)
            blocks.append(block)
        stacked = jnp.concatenate(blocks, axis=0).T
        spec[128 * g : 128 * (g + 1), :] = dot3(split(stacked), (dft_hi, dft_lo))
    sides = []
    for a in range(GZ):
        rest = arrived[pl.ds(3 * a + 2, GY, stride=3 * GZ), :]
        sides.append(rest + pltpu.roll(pltpu.roll(rest, 64, axis=1), 1, axis=0))
    blocks = []
    for i in range(KX):
        block = jnp.zeros((GY, 128), f32)
        for a in range(GZ):
            moved = pltpu.roll(sides[a], (8 * (a - i)) % 128, axis=1)
            block = jnp.where(lane // 8 == a, moved, block)
        blocks.append(block)
    stacked = jnp.concatenate(blocks, axis=0).T[:NZ]
    lines[...] = dot3(split(stacked), (dft_hi[:, :128], dft_lo[:, :128]))
    for g in range(2):
        total = [jnp.zeros((GY, 128), f32)] * 4
        for m in range(LY):
            c_main = fwd(0, m)
            c_partner = fwd(1, m)
            for k in range(4):
                row = 128 * g + 32 * k + m
                total[k] = total[k] + c_main * spec[row : row + 1, :128] + c_partner * spec[row : row + 1, 128:]
        for k in range(4):
            top[4 * g + k] = total[k]
    weight = fwd(0, 0)
    for s in range(half):
        for z in (s, NZ - 1 - s):
            right = weight * lines[z : z + 1, :]
            if z % LZ == 0:
                right = right + top[z // LZ]
            if s > 0:
                if z < half:
                    right = right + low[z : z + 1, :] * value[z - 1]
                else:
                    right = right + up[z : z + 1, :] * value[z + 1]
            value[z] = right * pivot[z]
    alpha = up[half - 1 : half, :] * pivot[half - 1]
    beta = low[half : half + 1, :] * pivot[half]
    below = (value[half - 1] + alpha * value[half]) / (1.0 - alpha * beta)
    above = value[half] + beta * below
    for s in range(half):
        for z in (half - 1 - s, half + s):
            if z < half:
                if s > 0:
                    below = value[z] + up[z : z + 1, :] * pivot[z] * below
                now = below
            else:
                if s > 0:
                    above = value[z] + low[z : z + 1, :] * pivot[z] * above
                now = above
            lines[z : z + 1, :] = jnp.sum(now * weight, axis=0, keepdims=True)
            if z % LZ == 0:
                top[z // LZ] = now
    for g in range(2):
        total = [jnp.zeros((LY, 128), f32)] * 4
        other = [jnp.zeros((LY, 128), f32)] * 4
        for j in range(GY):
            c_main = inv(0, j)
            c_partner = inv(1, j)
            for k in range(4):
                row = top[4 * g + k, j : j + 1, :]
                total[k] = total[k] + c_main * row
                other[k] = other[k] + c_partner * row
        for k in range(4):
            spec[128 * g + 32 * k : 128 * g + 32 * (k + 1), :128] = total[k]
            spec[128 * g + 32 * k : 128 * g + 32 * (k + 1), 128:] = other[k]
    for g in range(2):
        back[...] = dot3(split(spec[128 * g : 128 * (g + 1), :]), (idft_hi, idft_lo)).T
        for k in range(4):
            block = None
            for i in range(KX):
                moved = pltpu.roll(back[32 * i : 32 * (i + 1), :], (32 * (i - k)) % 128, axis=1)
                block = moved if block is None else jnp.where(lane // 32 == i, moved, block)
            a = 4 * g + k
            reply[pl.ds(3 * a, GY, stride=3 * GZ), :] = block
            if a > 0:
                reply[pl.ds(3 * (a - 1) + 1, GY, stride=3 * GZ), :] = block
    reply[pl.ds(3 * (GZ - 1) + 1, GY, stride=3 * GZ), :] = jnp.zeros((GY, 128), f32)
    rest = dot3(split(lines[...]), (idft_hi[:128, :], idft_lo[:128, :]))
    back[...] = jnp.concatenate([rest, rest], axis=0).T
    pieces = []
    for i in range(KX):
        piece = back[32 * i : 32 * (i + 1), :]
        pieces.append(jnp.where(lane < 64, piece, pltpu.roll(piece, GY - 1, axis=0)))
    for a in range(GZ):
        block = jnp.zeros((GY, 128), f32)
        for i in range(KX):
            moved = pltpu.roll(pieces[i], (8 * (i - a)) % 128, axis=1)
            block = jnp.where((lane % 64) // 8 == i, moved, block)
        reply[pl.ds(3 * a + 2, GY, stride=3 * GZ), :] = block


def restore(
    rows, arrived, kept, shared, block, pack, pressure, ends, result, out_sem,
):
    lower, upper, _ = wall_rows(rows, 256)
    small = sum(shared[512 + k * SMALL : 512 + (k + 1) * SMALL, :].astype(f32) for k in range(3))
    q_first, q_last, mask = (small[16 + k * LY : 16 + (k + 1) * LY] for k in range(3))
    for r in range(3):
        ends[128 * r : 128 * (r + 1), :] = arrived[pl.ds(r, DEV, stride=3), :].T
    lines = []
    for i in range(KX):
        floor = ends[i * LY : (i + 1) * LY, :]
        ceiling = ends[128 + i * LY : 128 + (i + 1) * LY, :]
        pivots = [None] + [block[i, (t - 1) * LY : t * LY, :] for t in range(1, LZ)]
        right = [None] * LZ
        near = [None] * LZ
        for t in range(1, LZ):
            near[t] = ends[256 + i * LZ + t : 256 + i * LZ + t + 1, :]
            far = ends[320 + i * LZ + t : 320 + i * LZ + t + 1, :]
            right[t] = kept[i, t * LY : (t + 1) * LY, :] + (q_first * near[t] + q_last * far)
        right[1] = right[1] + lower[1] * floor
        right[LZ - 1] = right[LZ - 1] + upper[LZ - 1] * ceiling
        inner = block_solve(right, pivots, lower, upper)
        layers = [floor] + [inner[t] + (1.0 - mask) * near[t] for t in range(1, LZ)]
        modes = jnp.concatenate(layers, axis=0)
        lines.append(sandwich(shared[:512, :], modes))

    def transform(line, wave):
        first = 512 * wave
        return dot3(line, (pack[first : first + 256, :], pack[first + 256 : first + 512, :]))

    minus = split(-lines[2])
    lines = [split(line) for line in lines]
    even = transform(lines[0], 0)
    odd = transform(lines[1], 1)
    copies = []
    for q in range(2):
        if q == 0:
            whole = even + odd
            swing = transform(lines[2], 2) + transform(lines[3], 3)
        else:
            whole = even - odd
            swing = transform(minus, 3) + transform(lines[3], 2)
        for k, piece in ((q, whole + swing), (q + 2, whole - swing)):
            here = pl.ds(256 * k, 256)
            result[:, :, 256 * k : 256 * (k + 1)] = piece.reshape(LZ, LY, 256)
            for part in range(2):
                where = pl.ds(part * LZ // 2, LZ // 2)
                copy = pltpu.make_async_copy(
                    result.at[where, :, here], pressure.at[where, :, here], out_sem.at[2 * k + part]
                )
                copy.start()
                copies.append(copy)
    for copy in copies:
        copy.wait()


def on_device(streamwise, spanwise, wall_normal, spacing):
    far = lambda x: pltpu.with_memory_space_constraint(x, pltpu.HBM)
    near = lambda x: pltpu.with_memory_space_constraint(x, pltpu.VMEM)
    pack, book, later = (jnp.asarray(part) for part in tables())
    pack, book = far(pack), far(book)
    vmem = pl.BlockSpec(memory_space=pltpu.VMEM)
    hbm = pl.BlockSpec(memory_space=pltpu.HBM)
    params = pltpu.CompilerParams(vmem_limit_bytes=50 * 2**20)
    shape = jax.ShapeDtypeStruct
    message, kept, heights, book, slabs, low, up, pivot, block, shared = pl.pallas_call(
        eliminate,
        out_shape=(
            pltpu.VMEM((3 * DEV, 128), f32),
            pltpu.VMEM((KX, LZ * LY, 256), f32),
            pltpu.VMEM((NZ, 128), f32),
            pltpu.VMEM((BOOK, 128), f32),
            pltpu.VMEM((512, 256), bf16),
            pltpu.VMEM((NZ, 128), f32),
            pltpu.VMEM((NZ, 128), f32),
            pltpu.VMEM((NZ, GY, 128), f32),
            pltpu.VMEM((KX, (LZ - 1) * LY, 256), f32),
            pltpu.VMEM((SHARED, 256), bf16),
        ),
        in_specs=[hbm] * 6,
        out_specs=(vmem,) * 10,
        scratch_shapes=[
            pltpu.SMEM((NZ,), f32),
            pltpu.VMEM((LZ, LY, NX), f32),
            pltpu.VMEM((LZ, LY, NX), f32),
            pltpu.VMEM((LZ, LY, NX), f32),
            pltpu.VMEM((8 * 256, 256), bf16),
            pltpu.VMEM((2 * ROWS[0], 256), bf16),
            pltpu.VMEM((2 * ROWS[0], 256), bf16),
            pltpu.VMEM((4 * ROWS[0], 256), bf16),
            pltpu.VMEM((2 * ROWS[1], 256), bf16),
            pltpu.VMEM((2 * ROWS[1], 256), bf16),
            pltpu.VMEM((4 * ROWS[1], 256), bf16),
            pltpu.VMEM((384, 256), f32),
            pltpu.SemaphoreType.DMA((LZ // 2, 3)),
            pltpu.SemaphoreType.DMA((7,)),
        ],
        compiler_params=params,
        name="eliminate",
    )(far(spacing), far(streamwise), far(spanwise), far(wall_normal), pack, book)
    axes = ("gy", "gz")
    trade = lambda x: lax.all_to_all(
        x.reshape(DEV, 1, 384), axes, split_axis=0, concat_axis=0, tiled=True
    ).reshape(3 * DEV, 128)
    arrived = trade(message)
    reply = pl.pallas_call(
        interface,
        out_shape=pltpu.VMEM((3 * DEV, 128), f32),
        in_specs=[vmem] * 6,
        out_specs=vmem,
        scratch_shapes=[
            pltpu.VMEM((NZ, GY, 128), f32),
            pltpu.VMEM((256, 256), f32),
            pltpu.VMEM((NZ, 128), f32),
            pltpu.VMEM((GZ, GY, 128), f32),
            pltpu.VMEM((128, 128), f32),
        ],
        compiler_params=params,
        name="interface",
    )(near(arrived), near(book), near(slabs), near(low), near(up), near(pivot))
    answered = trade(reply)
    return pl.pallas_call(
        restore,
        out_shape=shape((LZ, LY, NX), f32),
        in_specs=[vmem] * 6,
        out_specs=hbm,
        scratch_shapes=[
            pltpu.VMEM((384, 256), f32),
            pltpu.VMEM((LZ, LY, NX), f32),
            pltpu.SemaphoreType.DMA((8,)),
        ],
        compiler_params=params,
        name="restore",
    )(near(heights), near(answered), near(kept), near(shared), near(block), near(later))


def solution(mesh):
    placed = (P("gz", "gy", None), P("gz", "gy", None), P("gz", "gy", None), P())
    return jax.shard_map(
        on_device, mesh=mesh, in_specs=placed, out_specs=P("gz", "gy", None), check_vma=False
    )
```
